512 devices in a mesh: gx: 128 (over z, y_lo, x), gy: 4 (over y_hi, core).
Axes of the slice: x: 4, y: 4 (y_hi: 2, y_lo: 2; y = y_hi * 2 + y_lo), z: 16, core: 2. Of those that a mesh axis runs over, the one named last changes fastest.
Arguments:
- fine_cotangent: float32 [2, 2048, 1024], P(None, 'gx', 'gy'), may hold values from -6 to 6
- coarse_cotangent: float32 [2, 2048, 1024], P(None, 'gx', 'gy'), may hold values from -6 to 6
- upstream_x: int32 [3, 8], replicated, may hold values from -256 to 256, as said below
- upstream_y: int32 [3, 16], replicated, may hold values from -32 to 32, as said below
- fractions: float32 [3, 2], replicated, may hold values from 0.05 to 0.95
Outputs:
- difference: float32 [2, 2048, 1024], P(None, 'gx', 'gy')
The draws below stay inside these ranges and needn't reach their ends.
Inputs may be any that keep to these rules, and one draw needn't show every extreme that they name: `upstream_x`: each entry lies in -256 to 256; both ends occur in every draw. `upstream_y`: each entry lies in -32 to 32; both ends occur in every draw.
All inputs are finite; a program needn't handle non-finite values.
Results may differ from the reference program's by a relative error of at most 0.00002.
Values sent between devices are 32-bit elements; how exact they have to be, the bound alone decides.
A program may use at most 64 MiB of HBM per device.

```python
import jax
import jax.numpy as jnp

NZ = 2
LINE = 128
MAXDY = 32
MAXD = 256
NX = 2048
NY = 1024


def reach_both(key, total_count, largest):
    first_key, second_key = jax.random.split(key)
    values = jax.random.randint(first_key, (total_count,), -largest, largest + 1)
    ranking = jax.random.permutation(second_key, total_count)
    positions = jnp.arange(total_count)
    values = jnp.where(positions == ranking[0], largest, values)
    values = jnp.where(positions == ranking[1], -largest, values)
    return values.astype(jnp.int32)


def draw_upstream_x(key, part):
    return reach_both(jax.random.fold_in(key, 11), 3 * (NY // LINE), MAXD).reshape(3, NY // LINE)


def draw_upstream_y(key, part):
    return reach_both(jax.random.fold_in(key, 23), 3 * (NX // LINE), MAXDY).reshape(3, NX // LINE)


def level_of(key, dims, cuts, least, high):
    def one(dim, blocks):
        heights = jax.random.uniform(jax.random.fold_in(jax.random.fold_in(key, 6), dim), (blocks,), jnp.float32, least / len(cuts), high / len(cuts))
        return jnp.repeat(jnp.exp(heights), dims[dim] // blocks).reshape((-1,) + (1,) * (len(dims) - dim - 1))

    loudness = one(*cuts[0])
    for cut in cuts[1:]:
        loudness = loudness * one(*cut)
    return loudness


def normal_values(key, dims, deviation, reach, shards=(), held_as=jnp.bfloat16):
    factor_of = level_of(key, dims, shards, -0.22, 0.18) if shards else 1.0
    drawn = jax.random.normal(key, dims, jnp.float32) * deviation * factor_of
    return jnp.minimum(jnp.maximum(drawn, -reach), reach).astype(held_as)


def setup_inputs(seed: int = 0) -> dict:
    seeds = jax.random.split(jax.random.key(seed), 6)
    return {
        "fine_cotangent": normal_values(seeds[0], (NZ, NX, NY), 1.0, 6.0, ((1, 128), (2, 4)), jnp.float32),
        "coarse_cotangent": normal_values(seeds[1], (NZ, NX, NY), 1.0, 6.0, ((1, 128), (2, 4)), jnp.float32),
        "upstream_x": draw_upstream_x(jax.random.fold_in(seeds[5], 71), 0),
        "upstream_y": draw_upstream_y(jax.random.fold_in(seeds[5], 71), 0),
        "fractions": jnp.clip(jax.random.uniform(seeds[4], (3, 2), jnp.float32, 0.05, 0.95), 0.05, 0.95),
    }


def cubic_weights(fraction):
    position = 1.0 - fraction
    return (-position * (position - 1.0) * (position - 2.0) / 6.0,
            (position + 1.0) * (position - 1.0) * (position - 2.0) / 2.0,
            -(position + 1.0) * position * (position - 2.0) / 2.0,
            (position + 1.0) * position * (position - 1.0) / 6.0)


def sweep_axis(incoming, shifts, weights, block_axis, roll_axis, block_total):
    pieces = []
    for block_index in range(block_total):
        column = jax.lax.slice_in_dim(incoming, block_index * LINE, (block_index + 1) * LINE, axis=block_axis)
        summed = weights[0] * jnp.roll(column, -(shifts[block_index] + 2), axis=roll_axis)
        for tap_index in range(1, 4):
            summed = summed + weights[tap_index] * jnp.roll(column, -(shifts[block_index] + 2 - tap_index), axis=roll_axis)
        pieces.append(summed)
    return jnp.concatenate(pieces, axis=block_axis)


def adjoint_pass(incoming, upstream_x, upstream_y, fractions, pass_row):
    along_x = cubic_weights(fractions[pass_row, 0])
    along_y = cubic_weights(fractions[pass_row, 1])
    swept = sweep_axis(incoming, upstream_x[pass_row], along_x, 2, 1, NY // LINE)
    return sweep_axis(swept, upstream_y[pass_row], along_y, 1, 2, NX // LINE)


def reference(fine_cotangent, coarse_cotangent, upstream_x, upstream_y, fractions):
    fine_field = adjoint_pass(fine_cotangent, upstream_x, upstream_y, fractions, 1)
    fine_field = adjoint_pass(fine_field, upstream_x, upstream_y, fractions, 0)
    coarse_field = adjoint_pass(coarse_cotangent, upstream_x, upstream_y, fractions, 2)
    return fine_field - coarse_field
```

```python
import jax
import jax.numpy as jnp
from jax import lax
from jax.experimental import pallas as pl
from jax.experimental.pallas import tpu as pltpu
from jax.sharding import PartitionSpec as P

MESH = pl.DeviceIdType.MESH
PLANES = 16
GROUP = 8
RING = 4
HALF = 64
OWN = 17
WINDOW = 42


def cubic_weights(fraction):
    position = 1.0 - jnp.full((8, 128), fraction, jnp.float32)
    taps = (
        -position * (position - 1.0) * (position - 2.0) / 6.0,
        (position + 1.0) * (position - 1.0) * (position - 2.0) / 2.0,
        -(position + 1.0) * position * (position - 2.0) / 2.0,
        (position + 1.0) * position * (position - 1.0) / 6.0,
    )
    return taps[::-1]


def kernel(
    fine_hbm,
    coarse_hbm,
    upstream_x_hbm,
    upstream_y_hbm,
    fractions_hbm,
    out_ref,
    fine_ref,
    coarse_ref,
    upstream_x,
    upstream_y,
    fractions,
    packed_f,
    packed_c,
    window_1,
    window_0,
    window_2,
    rows,
    beside,
    swept_0,
    swept_2,
    back_f,
    back_c,
    sent,
    got,
    brought,
):
    arrivals = [
        pltpu.make_async_copy(source, target, brought.at[i])
        for i, (source, target) in enumerate(
            (
                (fine_hbm, fine_ref),
                (upstream_x_hbm, upstream_x),
                (upstream_y_hbm, upstream_y),
                (fractions_hbm, fractions),
                (coarse_hbm, coarse_ref),
            )
        )
    ]
    for arrival in arrivals:
        arrival.start()
    gx, gy = lax.axis_index("gx"), lax.axis_index("gy")
    plane, member = gx // GROUP, lax.rem(gx, GROUP)
    quarter, level = lax.rem(member, 4), member // 4
    lane = lax.broadcasted_iota(jnp.int32, (8, 128), 1)
    low = lane < HALF
    within = lax.rem(lane, HALF)

    def in_plane(other, gy_step=0):
        return plane * GROUP + other, lax.rem(gy + gy_step + RING, RING)

    def up_planes(step):
        return lax.rem(plane + step + PLANES, PLANES) * GROUP + member, gy

    def mate(step):
        return lax.rem(member + step, GROUP)

    def swap(tile):
        return pltpu.roll(tile, HALF, 1)

    def remote(source, target, channel, device, leave=None):
        leave = channel if leave is None else leave
        return pltpu.make_async_remote_copy(
            source, target, sent.at[leave], got.at[channel], device_id=device, device_id_type=MESH
        )

    def drain(ref, semaphores, channel):
        pltpu.make_async_copy(ref, ref, semaphores.at[channel]).wait()

    barrier = pltpu.get_barrier_semaphore()

    def greet(device):
        pl.semaphore_signal(barrier, inc=1, device_id=device, device_id_type=MESH)

    for step in (3, -3, 2, -2, 1, -1):
        greet(up_planes(step))
    for half in range(2):
        greet(in_plane(4 * half, 1))
        greet(in_plane(4 * half + 3, -1))
    for step in range(1, GROUP):
        greet(in_plane(mate(step)))
    edge = jnp.logical_or(quarter == 0, quarter == 3)

    def pack(field, packed):
        for lev in range(2):
            for block in range(2):
                columns = slice(128 * block, 128 * block + 128)
                upper = field[lev, 0:8, columns]
                lower = field[lev, 8:16, columns]
                packed[lev * 4 + 2 * block] = jnp.where(low, upper, swap(lower))
                packed[lev * 4 + 2 * block + 1] = jnp.where(low, swap(upper), lower)

    def transpose_start(packed, window, channel):
        for step in range(1, GROUP):
            other = mate(step)
            remote(packed.at[other], window.at[OWN + member], channel, in_plane(other)).start()
        window[OWN + member] = packed[member]

    def transpose_wait(window, channel):
        drain(window.at[pl.ds(0, 7)], got, channel)

    def planes_start(window, channel):
        own = window.at[pl.ds(OWN, 8)]
        remote(window.at[OWN + 7], window.at[0], channel, up_planes(3)).start()
        remote(window.at[OWN], window.at[WINDOW - 1], channel, up_planes(-3)).start()
        for step in (2, -2, 1, -1):
            remote(own, window.at[pl.ds(OWN - 8 * step, 8)], channel, up_planes(step)).start()

    def planes_wait(window, channel):
        drain(window.at[pl.ds(0, 34)], got, channel)

    def sweep_x(window, pass_row, target):
        shift = upstream_x[pass_row, 2 * gy + quarter // 2]
        weights = cubic_weights(fractions[0, pass_row])
        start = shift - 1 + 16 * OWN
        first, odd, inner = start // 16, lax.rem(start // 8, 2), lax.rem(start, 8)
        even_tiles = [window[first + i] for i in range(10)]
        swapped = [swap(tile) for tile in even_tiles]
        odd_tiles = [jnp.where(low, swapped[i], swapped[i + 1]) for i in range(9)]
        is_odd = jnp.full((8, 128), odd, jnp.int32) == 1
        lead = [jnp.where(is_odd, odd_tiles[i], even_tiles[i]) for i in range(9)]
        for i in range(8):
            rows[i, 0:8] = lead[i]
            rows[i, 8:16] = jnp.where(is_odd, even_tiles[i + 1], odd_tiles[i])
            rows[i, 16:24] = lead[i + 1]
        for i in range(8):
            summed = weights[0] * rows[i, pl.ds(inner, 8)]
            for tap in range(1, 4):
                summed = summed + weights[tap] * rows[i, pl.ds(inner + tap, 8)]
            target(i, summed)

    def sweep_y(pass_row, load, count):
        shift = upstream_y[pass_row, plane]
        weights = cubic_weights(fractions[1, pass_row])
        sums = [None] * count
        for tap in range(4):
            offset = shift - 1 + tap
            side = (offset >= 0).astype(jnp.int32)
            turn = offset + HALF * (1 - side)
            here = within + turn < HALF
            for i in range(count):
                cells = jnp.where(
                    here,
                    pltpu.roll(load(i, side), lax.rem(128 - turn, 128), 1),
                    pltpu.roll(load(i, side + 1), HALF - turn, 1),
                )
                term = weights[tap] * cells
                sums[i] = term if sums[i] is None else sums[i] + term
        return sums

    def back_start(swept, back, channel):
        for step in range(1, GROUP):
            other = mate(step)
            remote(swept.at[other], back.at[level, quarter + 1], channel, in_plane(other)).start()
        back[level, quarter + 1] = swept[member]

        @pl.when(edge)
        def _():
            side = jnp.where(quarter == 0, 5, 0)
            gy_step = jnp.where(quarter == 0, -1, 1)
            for other in range(GROUP):
                remote(swept.at[other], back.at[level, side], channel, in_plane(other, gy_step), channel + 2).start()

    def back_wait(channel):
        drain(window_0.at[pl.ds(0, 11)], got, channel)

    arrivals[0].wait()
    pack(fine_ref, packed_f)
    pl.semaphore_wait(barrier, jnp.where(edge, 21, 13))
    transpose_start(packed_f, window_1, 0)
    arrivals[4].wait()
    pack(coarse_ref, packed_c)
    transpose_start(packed_c, window_2, 1)
    for arrival in arrivals[1:4]:
        arrival.wait()
    transpose_wait(window_1, 0)
    planes_start(window_1, 2)
    planes_wait(window_1, 2)

    def keep_1(i, tile):
        beside[1, i] = tile

    sweep_x(window_1, 1, keep_1)
    right = jnp.where(quarter == 3, member - 3, member + 1)
    left = jnp.where(quarter == 0, member + 3, member - 1)
    remote(beside.at[1], beside.at[0], 3, in_plane(right, (quarter == 3).astype(jnp.int32))).start()
    remote(beside.at[1], beside.at[2], 3, in_plane(left, -(quarter == 0).astype(jnp.int32))).start()
    transpose_wait(window_2, 1)
    planes_start(window_2, 4)
    drain(window_1.at[pl.ds(0, 16)], got, 3)

    for i, tile in enumerate(sweep_y(1, lambda i, side: beside[side, i], 8)):
        window_0[OWN + i] = tile
    planes_start(window_0, 5)

    def keep_2(i, tile):
        swept_2[i] = tile

    planes_wait(window_2, 4)
    sweep_x(window_2, 2, keep_2)
    back_start(swept_2, back_c, 6)

    def keep_0(i, tile):
        swept_0[i] = tile

    planes_wait(window_0, 5)
    sweep_x(window_0, 0, keep_0)
    back_start(swept_0, back_f, 7)

    back_wait(6)
    coarse = sweep_y(2, lambda i, side: back_c[i // 4, lax.rem(i, 4) + side], 8)
    back_wait(7)
    fine = sweep_y(0, lambda i, side: back_f[i // 4, lax.rem(i, 4) + side], 8)
    tiles = [a - b for a, b in zip(fine, coarse)]
    for lev in range(2):
        for block in range(2):
            columns = slice(128 * block, 128 * block + 128)
            even, odd = tiles[lev * 4 + 2 * block], tiles[lev * 4 + 2 * block + 1]
            out_ref[lev, 0:8, columns] = jnp.where(low, even, swap(odd))
            out_ref[lev, 8:16, columns] = jnp.where(low, swap(even), odd)

    for channel in (0, 1):
        drain(window_0.at[pl.ds(0, 7)], sent, channel)
    for channel in (2, 4, 5):
        drain(window_0.at[pl.ds(0, 34)], sent, channel)
    drain(window_0.at[pl.ds(0, 16)], sent, 3)
    for channel in (6, 7):
        drain(window_0.at[pl.ds(0, 7)], sent, channel)

        @pl.when(edge)
        def _():
            drain(window_0.at[pl.ds(0, 8)], sent, channel + 2)


def local(fine_cotangent, coarse_cotangent, upstream_x, upstream_y, fractions):
    vmem = pl.BlockSpec(memory_space=pltpu.VMEM)
    anywhere = pl.BlockSpec(memory_space=pl.ANY)

    def tiles(*shape):
        return pltpu.VMEM((*shape, 8, 128), jnp.float32)

    return pl.pallas_call(
        kernel,
        out_shape=pltpu.VMEM(fine_cotangent.shape, jnp.float32),
        in_specs=[anywhere] * 5,
        out_specs=vmem,
        scratch_shapes=[
            pltpu.VMEM(fine_cotangent.shape, jnp.float32),
            pltpu.VMEM(fine_cotangent.shape, jnp.float32),
            pltpu.SMEM(upstream_x.shape, jnp.int32),
            pltpu.SMEM(upstream_y.shape, jnp.int32),
            pltpu.SMEM((2, 3), jnp.float32),
            tiles(GROUP),
            tiles(GROUP),
            tiles(WINDOW),
            tiles(WINDOW),
            tiles(WINDOW),
            pltpu.VMEM((8, 24, 128), jnp.float32),
            tiles(3, 8),
            tiles(8),
            tiles(8),
            tiles(2, 6),
            tiles(2, 6),
            pltpu.SemaphoreType.DMA((10,)),
            pltpu.SemaphoreType.DMA((8,)),
            pltpu.SemaphoreType.DMA((5,)),
        ],
        compiler_params=pltpu.CompilerParams(collective_id=0, has_side_effects=True),
    )(fine_cotangent, coarse_cotangent, upstream_x, upstream_y, fractions.T)


def solution(mesh):
    placed = (P(None, "gx", "gy"), P(None, "gx", "gy"), P(), P(), P())
    return jax.shard_map(
        local, mesh=mesh, in_specs=placed, out_specs=P(None, "gx", "gy"), check_vma=False
    )
```

```python
import jax
import jax.numpy as jnp
from jax import lax
from jax.experimental import pallas as pl
from jax.experimental.pallas import tpu as pltpu
from jax.sharding import PartitionSpec as P

MESH = pl.DeviceIdType.MESH
PLANES = 16
GROUP = 8
RING = 4
HALF = 64
OWN = 17
WINDOW = 42


def cubic_weights(fraction):
    position = 1.0 - jnp.full((8, 128), fraction, jnp.float32)
    taps = (
        -position * (position - 1.0) * (position - 2.0) / 6.0,
        (position + 1.0) * (position - 1.0) * (position - 2.0) / 2.0,
        -(position + 1.0) * position * (position - 2.0) / 2.0,
        (position + 1.0) * position * (position - 1.0) / 6.0,
    )
    return taps[::-1]


def kernel(
    fine_hbm,
    coarse_hbm,
    upstream_x_hbm,
    upstream_y_hbm,
    fractions_hbm,
    out_ref,
    fine_ref,
    coarse_ref,
    upstream_x,
    upstream_y,
    fractions,
    packed_f,
    packed_c,
    cells,
    edges,
    ahead,
    fringe,
    window_1,
    window_0,
    window_2,
    rows,
    swept_0,
    swept_2,
    back_f,
    back_c,
    sent,
    got,
    brought,
):
    arrivals = [
        pltpu.make_async_copy(source, target, brought.at[i])
        for i, (source, target) in enumerate(
            (
                (fine_hbm, fine_ref),
                (upstream_x_hbm, upstream_x),
                (upstream_y_hbm, upstream_y),
                (fractions_hbm, fractions),
                (coarse_hbm, coarse_ref),
            )
        )
    ]
    for arrival in arrivals:
        arrival.start()
    gx, gy = lax.axis_index("gx"), lax.axis_index("gy")
    plane, member = gx // GROUP, lax.rem(gx, GROUP)
    quarter, level = lax.rem(member, 4), member // 4
    lane = lax.broadcasted_iota(jnp.int32, (8, 128), 1)
    low = lane < HALF
    within = lax.rem(lane, HALF)

    def in_plane(other, gy_step=0):
        return plane * GROUP + other, lax.rem(gy + gy_step + RING, RING)

    def up_planes(step):
        return lax.rem(plane + step + PLANES, PLANES) * GROUP + member, gy

    def mate(step):
        return lax.rem(member + step, GROUP)

    def swap(tile):
        return pltpu.roll(tile, HALF, 1)

    def remote(source, target, channel, device, leave=None):
        leave = channel if leave is None else leave
        return pltpu.make_async_remote_copy(
            source, target, sent.at[leave], got.at[channel], device_id=device, device_id_type=MESH
        )

    def drain(ref, semaphores, channel):
        pltpu.make_async_copy(ref, ref, semaphores.at[channel]).wait()

    barrier = pltpu.get_barrier_semaphore()

    def greet(device):
        pl.semaphore_signal(barrier, inc=1, device_id=device, device_id_type=MESH)

    edge = jnp.logical_or(quarter == 0, quarter == 3)
    outward = jnp.where(quarter == 0, -1, 1)
    for step in (3, -3, 2, -2, 1, -1):
        greet(up_planes(step))

    @pl.when(edge)
    def _():
        for other in range(GROUP):
            greet(in_plane(other, outward))

    for step in range(1, GROUP):
        greet(in_plane(mate(step)))

    def pack(field, place):
        for lev in range(2):
            for block in range(2):
                columns = slice(128 * block, 128 * block + 128)
                upper = field[lev, 0:8, columns]
                lower = field[lev, 8:16, columns]
                place(lev, 2 * block, jnp.where(low, upper, swap(lower)))
                place(lev, 2 * block + 1, jnp.where(low, swap(upper), lower))

    def transpose_start(packed, window, channel):
        for step in range(1, GROUP):
            other = mate(step)
            remote(packed.at[other], window.at[OWN + member], channel, in_plane(other)).start()
        window[OWN + member] = packed[member]

    def transpose_wait(window, channel):
        drain(window.at[pl.ds(0, 7)], got, channel)

    def planes_start(window, channel):
        own = window.at[pl.ds(OWN, 8)]
        remote(window.at[OWN + 7], window.at[0], channel, up_planes(3)).start()
        remote(window.at[OWN], window.at[WINDOW - 1], channel, up_planes(-3)).start()
        for step in (2, -2, 1, -1):
            remote(own, window.at[pl.ds(OWN - 8 * step, 8)], channel, up_planes(step)).start()

    def planes_wait(window, channel):
        drain(window.at[pl.ds(0, 34)], got, channel)

    def sweep_x(load, pass_row, block):
        shift = upstream_x[pass_row, block]
        weights = cubic_weights(fractions[0, pass_row])
        start = shift - 1 + 16 * OWN
        first, odd, inner = start // 16, lax.rem(start // 8, 2), lax.rem(start, 8)
        even_tiles = [load(first + i) for i in range(10)]
        swapped = [swap(tile) for tile in even_tiles]
        odd_tiles = [jnp.where(low, swapped[i], swapped[i + 1]) for i in range(9)]
        is_odd = jnp.full((8, 128), odd, jnp.int32) == 1
        lead = [jnp.where(is_odd, odd_tiles[i], even_tiles[i]) for i in range(9)]
        for i in range(8):
            rows[i, 0:8] = lead[i]
            rows[i, 8:16] = jnp.where(is_odd, even_tiles[i + 1], odd_tiles[i])
            rows[i, 16:24] = lead[i + 1]
        sums = []
        for i in range(8):
            summed = weights[0] * rows[i, pl.ds(inner, 8)]
            for tap in range(1, 4):
                summed = summed + weights[tap] * rows[i, pl.ds(inner + tap, 8)]
            sums.append(summed)
        return sums

    def shifted_cells(load, i, offset):
        side = (offset >= 0).astype(jnp.int32)
        turn = offset + HALF * (1 - side)
        return jnp.where(
            within + turn < HALF,
            pltpu.roll(load(i, side), lax.rem(128 - turn, 128), 1),
            pltpu.roll(load(i, side + 1), HALF - turn, 1),
        )

    border = HALF * lax.rem(quarter, 2)
    low_block = lax.rem(2 * gy + (quarter + 1) // 2 - 1 + 2 * RING, 2 * RING)
    high_block = lax.rem(low_block + 1, 2 * RING)

    def crossing_of(to_plane):
        return border - upstream_y[1, to_plane] - 2

    def sweep_y_ahead(to_plane, tiles, target, at):
        shift = upstream_y[1, to_plane]
        crossing = crossing_of(to_plane)
        upper_columns = within > crossing + 2
        spare = jnp.zeros((8, 128), jnp.float32)
        parts = []
        for tap, weight in enumerate(cubic_weights(fractions[1, 1])):
            offset = shift - 1 + tap
            split = jnp.logical_and(within + offset >= border, jnp.logical_not(upper_columns))
            parts.append((offset, jnp.where(split, 0.0, weight), jnp.where(split, weight, 0.0)))
        for n, i in enumerate(tiles):
            main = jnp.zeros((8, 128), jnp.float32)
            second = jnp.zeros((8, 128), jnp.float32)
            for offset, first_weight, second_weight in parts:
                moved = shifted_cells(lambda i, side: cells[i, side], i, offset)
                main = main + first_weight * moved
                second = second + second_weight * moved
            target[at + n] = main
            spare = spare + pltpu.roll(second, lax.rem(8 * i - crossing + 256, 128), 1)
        target[at + len(tiles)] = spare

    def sweep_x_both():
        crossing = crossing_of(plane)
        upper_columns = within > crossing + 2
        both = jnp.logical_and(within >= crossing, within <= crossing + 2)

        def load_low(i):
            place = 9 * ((i + 7) // 8) + lax.rem(i + 7, 8)
            return jnp.where(upper_columns, 0.0, window_1[place])

        def load_high(i):
            level_plane, inside = (i + 7) // 8, lax.rem(i + 7, 8)
            spare = window_1[jnp.where(level_plane == 6, 55, 9 * level_plane + 8)]
            spare = pltpu.roll(spare, lax.rem(crossing - 8 * inside + 256, 128), 1)
            return jnp.where(upper_columns, window_1[9 * level_plane + inside], jnp.where(both, spare, 0.0))

        low_part = sweep_x(load_low, 1, low_block)
        high_part = sweep_x(load_high, 1, high_block)
        return [a + b for a, b in zip(low_part, high_part)]

    def sweep_y(pass_row, load, count):
        shift = upstream_y[pass_row, plane]
        weights = cubic_weights(fractions[1, pass_row])
        sums = [None] * count
        for tap in range(4):
            for i in range(count):
                term = weights[tap] * shifted_cells(load, i, shift - 1 + tap)
                sums[i] = term if sums[i] is None else sums[i] + term
        return sums

    def back_start(swept, back, channel):
        for step in range(1, GROUP):
            other = mate(step)
            remote(swept.at[other], back.at[level, quarter + 1], channel, in_plane(other)).start()
        back[level, quarter + 1] = swept[member]

        @pl.when(edge)
        def _():
            side = jnp.where(quarter == 0, 5, 0)
            for other in range(GROUP):
                remote(swept.at[other], back.at[level, side], channel, in_plane(other, outward), channel + 2).start()

    def back_wait(channel):
        drain(window_0.at[pl.ds(0, 11)], got, channel)

    def place_f(lev, part, tile):
        packed_f[lev, part + 1] = tile

    def place_c(lev, part, tile):
        packed_c[4 * lev + part] = tile

    for lev in range(2):
        packed_f[lev, 0] = jnp.zeros((8, 128), jnp.float32)
        packed_f[lev, 5] = jnp.zeros((8, 128), jnp.float32)
    arrivals[0].wait()
    pack(fine_ref, place_f)
    pl.semaphore_wait(barrier, 17)

    for lev in range(2):
        remote(packed_f.at[lev, 4], edges.at[member], 3, in_plane(4 * lev, 1)).start()
        remote(packed_f.at[lev, 1], edges.at[member], 3, in_plane(4 * lev + 3, -1)).start()
    for step in range(1, GROUP):
        other = mate(step)
        source = packed_f.at[other // 4, pl.ds(lax.rem(other, 4), 3)]
        remote(source, cells.at[member], 0, in_plane(other)).start()
    cells[member] = packed_f[level, pl.ds(quarter, 3)]
    arrivals[4].wait()
    pack(coarse_ref, place_c)
    transpose_start(packed_c, window_2, 1)
    for arrival in arrivals[1:4]:
        arrival.wait()
    drain(cells.at[pl.ds(0, 7)], got, 0)

    @pl.when(edge)
    def _():
        drain(edges, got, 3)
        side = jnp.where(quarter == 0, 0, 2)
        for i in range(8):
            cells[i, side] = edges[i]

    def to(step):
        return lax.rem(plane + step + PLANES, PLANES)

    sweep_y_ahead(to(3), (7,), fringe, 0)
    remote(fringe.at[pl.ds(0, 2)], window_1.at[pl.ds(7, 2)], 2, up_planes(3)).start()
    sweep_y_ahead(to(-3), (0,), fringe, 2)
    remote(fringe.at[pl.ds(2, 2)], window_1.at[pl.ds(54, 2)], 2, up_planes(-3)).start()
    for n, step in enumerate((2, -2, 1, -1)):
        sweep_y_ahead(to(step), range(8), ahead, 9 * n)
        target = window_1.at[pl.ds(9 * (3 - step), 9)]
        remote(ahead.at[pl.ds(9 * n, 9)], target, 2, up_planes(step)).start()
    sweep_y_ahead(plane, range(8), window_1, 27)
    transpose_wait(window_2, 1)
    planes_start(window_2, 4)
    drain(window_1.at[pl.ds(0, 40)], got, 2)

    for i, tile in enumerate(sweep_x_both()):
        window_0[OWN + i] = tile
    planes_start(window_0, 5)

    own_block = 2 * gy + quarter // 2
    planes_wait(window_2, 4)
    for i, tile in enumerate(sweep_x(lambda i: window_2[i], 2, own_block)):
        swept_2[i] = tile
    back_start(swept_2, back_c, 6)

    planes_wait(window_0, 5)
    for i, tile in enumerate(sweep_x(lambda i: window_0[i], 0, own_block)):
        swept_0[i] = tile
    back_start(swept_0, back_f, 7)

    back_wait(6)
    coarse = sweep_y(2, lambda i, side: back_c[i // 4, lax.rem(i, 4) + side], 8)
    back_wait(7)
    fine = sweep_y(0, lambda i, side: back_f[i // 4, lax.rem(i, 4) + side], 8)
    tiles = [a - b for a, b in zip(fine, coarse)]
    for lev in range(2):
        for block in range(2):
            columns = slice(128 * block, 128 * block + 128)
            even, odd = tiles[lev * 4 + 2 * block], tiles[lev * 4 + 2 * block + 1]
            out_ref[lev, 0:8, columns] = jnp.where(low, even, swap(odd))
            out_ref[lev, 8:16, columns] = jnp.where(low, swap(even), odd)

    drain(cells.at[pl.ds(0, 7)], sent, 0)
    drain(window_0.at[pl.ds(0, 7)], sent, 1)
    drain(window_0.at[pl.ds(0, 4)], sent, 3)
    drain(window_1.at[pl.ds(0, 40)], sent, 2)
    for channel in (4, 5):
        drain(window_0.at[pl.ds(0, 34)], sent, channel)
    for channel in (6, 7):
        drain(window_0.at[pl.ds(0, 7)], sent, channel)

        @pl.when(edge)
        def _():
            drain(window_0.at[pl.ds(0, 8)], sent, channel + 2)


def local(fine_cotangent, coarse_cotangent, upstream_x, upstream_y, fractions):
    vmem = pl.BlockSpec(memory_space=pltpu.VMEM)
    anywhere = pl.BlockSpec(memory_space=pl.ANY)

    def tiles(*shape):
        return pltpu.VMEM((*shape, 8, 128), jnp.float32)

    return pl.pallas_call(
        kernel,
        out_shape=pltpu.VMEM(fine_cotangent.shape, jnp.float32),
        in_specs=[anywhere] * 5,
        out_specs=vmem,
        scratch_shapes=[
            pltpu.VMEM(fine_cotangent.shape, jnp.float32),
            pltpu.VMEM(fine_cotangent.shape, jnp.float32),
            pltpu.SMEM(upstream_x.shape, jnp.int32),
            pltpu.SMEM(upstream_y.shape, jnp.int32),
            pltpu.SMEM((2, 3), jnp.float32),
            tiles(2, 6),
            tiles(GROUP),
            tiles(8, 3),
            tiles(8),
            tiles(36),
            tiles(4),
            tiles(63),
            tiles(WINDOW),
            tiles(WINDOW),
            pltpu.VMEM((8, 24, 128), jnp.float32),
            tiles(8),
            tiles(8),
            tiles(2, 6),
            tiles(2, 6),
            pltpu.SemaphoreType.DMA((10,)),
            pltpu.SemaphoreType.DMA((8,)),
            pltpu.SemaphoreType.DMA((5,)),
        ],
        compiler_params=pltpu.CompilerParams(collective_id=0, has_side_effects=True),
    )(fine_cotangent, coarse_cotangent, upstream_x, upstream_y, fractions.T)


def solution(mesh):
    placed = (P(None, "gx", "gy"), P(None, "gx", "gy"), P(), P(), P())
    return jax.shard_map(
        local, mesh=mesh, in_specs=placed, out_specs=P(None, "gx", "gy"), check_vma=False
    )
```

```python
import jax
import jax.numpy as jnp
from jax import lax
from jax.experimental import pallas as pl
from jax.experimental.pallas import tpu as pltpu
from jax.sharding import PartitionSpec as P

MESH = pl.DeviceIdType.MESH
PLANES = 16
GROUP = 8
RING = 4
HALF = 64
OWN = 17
WINDOW = 42


def cubic_weights(fraction):
    position = 1.0 - jnp.full((8, 128), fraction, jnp.float32)
    taps = (
        -position * (position - 1.0) * (position - 2.0) / 6.0,
        (position + 1.0) * (position - 1.0) * (position - 2.0) / 2.0,
        -(position + 1.0) * position * (position - 2.0) / 2.0,
        (position + 1.0) * position * (position - 1.0) / 6.0,
    )
    return taps[::-1]


def kernel(
    fine_hbm,
    coarse_hbm,
    upstream_x_hbm,
    upstream_y_hbm,
    fractions_hbm,
    out_ref,
    fine_ref,
    coarse_ref,
    upstream_x,
    upstream_y,
    fractions,
    packed_f,
    packed_c,
    cells,
    edges,
    ahead,
    fringe,
    window_1,
    ready,
    strewn,
    swept_0,
    window_2,
    rows,
    swept_2,
    back_f,
    back_c,
    sent,
    got,
    brought,
):
    arrivals = [
        pltpu.make_async_copy(source, target, brought.at[i])
        for i, (source, target) in enumerate(
            (
                (fine_hbm, fine_ref),
                (upstream_x_hbm, upstream_x),
                (upstream_y_hbm, upstream_y),
                (fractions_hbm, fractions),
                (coarse_hbm, coarse_ref),
            )
        )
    ]
    for arrival in arrivals:
        arrival.start()
    gx, gy = lax.axis_index("gx"), lax.axis_index("gy")
    plane, member = gx // GROUP, lax.rem(gx, GROUP)
    quarter, level = lax.rem(member, 4), member // 4
    lane = lax.broadcasted_iota(jnp.int32, (8, 128), 1)
    low = lane < HALF
    within = lax.rem(lane, HALF)

    def in_plane(other, gy_step=0):
        return plane * GROUP + other, lax.rem(gy + gy_step + RING, RING)

    def up_planes(step):
        return lax.rem(plane + step + PLANES, PLANES) * GROUP + member, gy

    def mate(step):
        return lax.rem(member + step, GROUP)

    def swap(tile):
        return pltpu.roll(tile, HALF, 1)

    def remote(source, target, channel, device, leave=None):
        leave = channel if leave is None else leave
        return pltpu.make_async_remote_copy(
            source, target, sent.at[leave], got.at[channel], device_id=device, device_id_type=MESH
        )

    def drain(ref, semaphores, channel):
        pltpu.make_async_copy(ref, ref, semaphores.at[channel]).wait()

    barrier = pltpu.get_barrier_semaphore()

    def greet(device):
        pl.semaphore_signal(barrier, inc=1, device_id=device, device_id_type=MESH)

    edge = jnp.logical_or(quarter == 0, quarter == 3)
    outward = jnp.where(quarter == 0, -1, 1)
    for step in (3, -3, 2, -2, 1, -1):
        greet(up_planes(step))

    @pl.when(edge)
    def _():
        for other in range(GROUP):
            greet(in_plane(other, outward))

    for step in range(1, GROUP):
        greet(in_plane(mate(step)))

    def pack(field, place):
        for lev in range(2):
            for block in range(2):
                columns = slice(128 * block, 128 * block + 128)
                upper = field[lev, 0:8, columns]
                lower = field[lev, 8:16, columns]
                place(lev, 2 * block, jnp.where(low, upper, swap(lower)))
                place(lev, 2 * block + 1, jnp.where(low, swap(upper), lower))

    def transpose_start(packed, window, channel):
        for step in range(1, GROUP):
            other = mate(step)
            remote(packed.at[other], window.at[OWN + member], channel, in_plane(other)).start()
        window[OWN + member] = packed[member]

    def transpose_wait(window, channel):
        drain(window.at[pl.ds(0, 7)], got, channel)

    def planes_start(window, channel):
        own = window.at[pl.ds(OWN, 8)]
        remote(window.at[OWN + 7], window.at[0], channel, up_planes(3)).start()
        remote(window.at[OWN], window.at[WINDOW - 1], channel, up_planes(-3)).start()
        for step in (2, -2, 1, -1):
            remote(own, window.at[pl.ds(OWN - 8 * step, 8)], channel, up_planes(step)).start()

    def planes_wait(window, channel):
        drain(window.at[pl.ds(0, 34)], got, channel)

    def sweep_x(load, pass_row, block):
        shift = upstream_x[pass_row, block]
        weights = cubic_weights(fractions[0, pass_row])
        start = shift - 1 + 16 * OWN
        first = start // 16
        return slide([load(first + i) for i in range(10)], start, weights)

    def slide(even_tiles, start, weights):
        count = len(even_tiles) - 2
        odd, inner = lax.rem(start // 8, 2), lax.rem(start, 8)
        swapped = [swap(tile) for tile in even_tiles]
        odd_tiles = [jnp.where(low, swapped[i], swapped[i + 1]) for i in range(count + 1)]
        is_odd = jnp.full((8, 128), odd, jnp.int32) == 1
        lead = [jnp.where(is_odd, odd_tiles[i], even_tiles[i]) for i in range(count + 1)]
        for i in range(count):
            rows[i, 0:8] = lead[i]
            rows[i, 8:16] = jnp.where(is_odd, even_tiles[i + 1], odd_tiles[i])
            rows[i, 16:24] = lead[i + 1]
        sums = []
        for i in range(count):
            summed = weights[0] * rows[i, pl.ds(inner, 8)]
            for tap in range(1, 4):
                summed = summed + weights[tap] * rows[i, pl.ds(inner + tap, 8)]
            sums.append(summed)
        return sums

    def shifted_cells(load, i, offset):
        side = (offset >= 0).astype(jnp.int32)
        turn = offset + HALF * (1 - side)
        return jnp.where(
            within + turn < HALF,
            pltpu.roll(load(i, side), lax.rem(128 - turn, 128), 1),
            pltpu.roll(load(i, side + 1), HALF - turn, 1),
        )

    border = HALF * lax.rem(quarter, 2)
    low_block = lax.rem(2 * gy + (quarter + 1) // 2 - 1 + 2 * RING, 2 * RING)
    high_block = lax.rem(low_block + 1, 2 * RING)

    def crossing_of(to_plane):
        return border - upstream_y[1, to_plane] - 2

    def sweep_y_ahead(to_plane, tiles, target, at):
        shift = upstream_y[1, to_plane]
        crossing = crossing_of(to_plane)
        upper_columns = within > crossing + 2
        spare = jnp.zeros((8, 128), jnp.float32)
        parts = []
        for tap, weight in enumerate(cubic_weights(fractions[1, 1])):
            offset = shift - 1 + tap
            split = jnp.logical_and(within + offset >= border, jnp.logical_not(upper_columns))
            parts.append((offset, jnp.where(split, 0.0, weight), jnp.where(split, weight, 0.0)))
        for n, i in enumerate(tiles):
            main = jnp.zeros((8, 128), jnp.float32)
            second = jnp.zeros((8, 128), jnp.float32)
            for offset, first_weight, second_weight in parts:
                moved = shifted_cells(lambda i, side: cells[i, side], i, offset)
                main = main + first_weight * moved
                second = second + second_weight * moved
            target[at + n] = main
            spare = spare + pltpu.roll(second, lax.rem(8 * i - crossing + 256, 128), 1)
        target[at + len(tiles)] = spare

    def sweep_x_both():
        crossing = crossing_of(plane)
        upper_columns = within > crossing + 2
        both = jnp.logical_and(within >= crossing, within <= crossing + 2)

        def load_low(i):
            place = 9 * ((i + 7) // 8) + lax.rem(i + 7, 8)
            return jnp.where(upper_columns, 0.0, window_1[place])

        def load_high(i):
            level_plane, inside = (i + 7) // 8, lax.rem(i + 7, 8)
            spare = window_1[jnp.where(level_plane == 6, 55, 9 * level_plane + 8)]
            spare = pltpu.roll(spare, lax.rem(crossing - 8 * inside + 256, 128), 1)
            return jnp.where(upper_columns, window_1[9 * level_plane + inside], jnp.where(both, spare, 0.0))

        low_part = sweep_x(load_low, 1, low_block)
        high_part = sweep_x(load_high, 1, high_block)
        return [a + b for a, b in zip(low_part, high_part)]

    def sweep_y(pass_row, load, count):
        shift = upstream_y[pass_row, plane]
        weights = cubic_weights(fractions[1, pass_row])
        sums = [None] * count
        for tap in range(4):
            for i in range(count):
                term = weights[tap] * shifted_cells(load, i, shift - 1 + tap)
                sums[i] = term if sums[i] is None else sums[i] + term
        return sums

    def back_start(swept, back, channel):
        for step in range(1, GROUP):
            other = mate(step)
            remote(swept.at[other], back.at[level, quarter + 1], channel, in_plane(other)).start()
        back[level, quarter + 1] = swept[member]

        @pl.when(edge)
        def _():
            side = jnp.where(quarter == 0, 5, 0)
            for other in range(GROUP):
                remote(swept.at[other], back.at[level, side], channel, in_plane(other, outward), channel + 2).start()

    def back_wait(channel):
        drain(window_2.at[pl.ds(0, 11)], got, channel)

    blank = jnp.zeros((8, 128), jnp.float32)
    for i in (0, 1, 10, 11):
        ready[i] = blank
    for i in range(76):
        strewn[i] = blank

    @pl.when(jnp.logical_and(member > 0, member < 7))
    def _():
        for lev in range(2):
            for part in range(6):
                back_f[lev, part, 5] = blank

    def place_f(lev, part, tile):
        packed_f[lev, part + 1] = tile

    def place_c(lev, part, tile):
        packed_c[4 * lev + part] = tile

    for lev in range(2):
        packed_f[lev, 0] = jnp.zeros((8, 128), jnp.float32)
        packed_f[lev, 5] = jnp.zeros((8, 128), jnp.float32)
    arrivals[0].wait()
    pack(fine_ref, place_f)
    pl.semaphore_wait(barrier, 17)

    for lev in range(2):
        remote(packed_f.at[lev, 4], edges.at[member], 3, in_plane(4 * lev, 1)).start()
        remote(packed_f.at[lev, 1], edges.at[member], 3, in_plane(4 * lev + 3, -1)).start()
    for step in range(1, GROUP):
        other = mate(step)
        source = packed_f.at[other // 4, pl.ds(lax.rem(other, 4), 3)]
        remote(source, cells.at[member], 0, in_plane(other)).start()
    cells[member] = packed_f[level, pl.ds(quarter, 3)]
    arrivals[4].wait()
    pack(coarse_ref, place_c)
    transpose_start(packed_c, window_2, 1)
    for arrival in arrivals[1:4]:
        arrival.wait()
    drain(cells.at[pl.ds(0, 7)], got, 0)

    @pl.when(edge)
    def _():
        drain(edges, got, 3)
        side = jnp.where(quarter == 0, 0, 2)
        for i in range(8):
            cells[i, side] = edges[i]

    def to(step):
        return lax.rem(plane + step + PLANES, PLANES)

    sweep_y_ahead(to(3), (7,), fringe, 0)
    remote(fringe.at[pl.ds(0, 2)], window_1.at[pl.ds(7, 2)], 2, up_planes(3)).start()
    sweep_y_ahead(to(-3), (0,), fringe, 2)
    remote(fringe.at[pl.ds(2, 2)], window_1.at[pl.ds(54, 2)], 2, up_planes(-3)).start()
    for n, step in enumerate((2, -2, 1, -1)):
        sweep_y_ahead(to(step), range(8), ahead, 9 * n)
        target = window_1.at[pl.ds(9 * (3 - step), 9)]
        remote(ahead.at[pl.ds(9 * n, 9)], target, 2, up_planes(step)).start()
    sweep_y_ahead(plane, range(8), window_1, 27)
    transpose_wait(window_2, 1)
    planes_start(window_2, 4)
    own_block = 2 * gy + quarter // 2
    drain(window_1.at[pl.ds(0, 40)], got, 2)

    for i, tile in enumerate(sweep_x_both()):
        ready[2 + i] = tile
    start = upstream_x[0, own_block] - 1 + 16 * OWN
    parts = slide([ready[i] for i in range(12)], start, cubic_weights(fractions[0, 0]))
    for i, tile in enumerate(parts):
        strewn[32 + i] = tile
    for i in range(WINDOW):
        swept_0[i] = strewn[start // 16 + i]

    def scatter_start(step, others, slot):
        def start_at(gy_step, side, leave, skip):
            for other in others:
                target_plane = lax.rem(plane - step + PLANES, PLANES)
                copy = remote(
                    swept_0.at[OWN - 8 * step + other],
                    back_f.at[level, side, slot],
                    7,
                    (target_plane * GROUP + other, lax.rem(gy + gy_step + RING, RING)),
                    leave,
                )
                if skip:
                    pl.when(other != member)(copy.start)
                else:
                    copy.start()

        @pl.when(edge)
        def _():
            start_at(outward, jnp.where(quarter == 0, 5, 0), 9, False)

        start_at(0, quarter + 1, 7, step == 0)

    scatter_start(3, (7,), 5)
    scatter_start(-3, (0,), 5)
    for step in (2, -2, 1, -1, 0):
        scatter_start(step, range(GROUP), step + 2)
    back_f[level, quarter + 1, 2] = swept_0[OWN + member]

    planes_wait(window_2, 4)
    for i, tile in enumerate(sweep_x(lambda i: window_2[i], 2, own_block)):
        swept_2[i] = tile
    back_start(swept_2, back_c, 6)

    back_wait(6)
    coarse = sweep_y(2, lambda i, side: back_c[i // 4, lax.rem(i, 4) + side], 8)

    outer = jnp.logical_or(member == 0, member == 7)

    @pl.when(outer)
    def _():
        drain(strewn.at[pl.ds(0, 71)], got, 7)

    @pl.when(jnp.logical_not(outer))
    def _():
        drain(strewn.at[pl.ds(0, 59)], got, 7)

    for lev in range(2):
        for part in range(6):
            total = back_f[lev, part, 0]
            for slot in range(1, 6):
                total = total + back_f[lev, part, slot]
            ready[lev * 6 + part] = total
    fine = sweep_y(0, lambda i, side: ready[6 * (i // 4) + lax.rem(i, 4) + side], 8)
    tiles = [a - b for a, b in zip(fine, coarse)]
    for lev in range(2):
        for block in range(2):
            columns = slice(128 * block, 128 * block + 128)
            even, odd = tiles[lev * 4 + 2 * block], tiles[lev * 4 + 2 * block + 1]
            out_ref[lev, 0:8, columns] = jnp.where(low, even, swap(odd))
            out_ref[lev, 8:16, columns] = jnp.where(low, swap(even), odd)

    drain(cells.at[pl.ds(0, 7)], sent, 0)
    drain(window_2.at[pl.ds(0, 7)], sent, 1)
    drain(window_2.at[pl.ds(0, 4)], sent, 3)
    drain(window_1.at[pl.ds(0, 40)], sent, 2)
    drain(window_2.at[pl.ds(0, 34)], sent, 4)
    drain(window_2.at[pl.ds(0, 7)], sent, 6)
    drain(window_2.at[pl.ds(0, 41)], sent, 7)

    @pl.when(edge)
    def _():
        drain(window_2.at[pl.ds(0, 8)], sent, 8)
        drain(window_2.at[pl.ds(0, 42)], sent, 9)


def local(fine_cotangent, coarse_cotangent, upstream_x, upstream_y, fractions):
    vmem = pl.BlockSpec(memory_space=pltpu.VMEM)
    anywhere = pl.BlockSpec(memory_space=pl.ANY)

    def tiles(*shape):
        return pltpu.VMEM((*shape, 8, 128), jnp.float32)

    return pl.pallas_call(
        kernel,
        out_shape=pltpu.VMEM(fine_cotangent.shape, jnp.float32),
        in_specs=[anywhere] * 5,
        out_specs=vmem,
        scratch_shapes=[
            pltpu.VMEM(fine_cotangent.shape, jnp.float32),
            pltpu.VMEM(fine_cotangent.shape, jnp.float32),
            pltpu.SMEM(upstream_x.shape, jnp.int32),
            pltpu.SMEM(upstream_y.shape, jnp.int32),
            pltpu.SMEM((2, 3), jnp.float32),
            tiles(2, 6),
            tiles(GROUP),
            tiles(8, 3),
            tiles(8),
            tiles(36),
            tiles(4),
            tiles(63),
            tiles(12),
            tiles(76),
            tiles(WINDOW),
            tiles(WINDOW),
            pltpu.VMEM((10, 24, 128), jnp.float32),
            tiles(8),
            tiles(2, 6, 6),
            tiles(2, 6),
            pltpu.SemaphoreType.DMA((10,)),
            pltpu.SemaphoreType.DMA((8,)),
            pltpu.SemaphoreType.DMA((5,)),
        ],
        compiler_params=pltpu.CompilerParams(collective_id=0, has_side_effects=True),
    )(fine_cotangent, coarse_cotangent, upstream_x, upstream_y, fractions.T)


def solution(mesh):
    placed = (P(None, "gx", "gy"), P(None, "gx", "gy"), P(), P(), P())
    return jax.shard_map(
        local, mesh=mesh, in_specs=placed, out_specs=P(None, "gx", "gy"), check_vma=False
    )
```

```python
import jax
import jax.numpy as jnp
from jax import lax
from jax.experimental import pallas as pl
from jax.experimental.pallas import tpu as pltpu
from jax.sharding import PartitionSpec as P

MESH = pl.DeviceIdType.MESH
PLANES = 16
GROUP = 8
RING = 4
HALF = 64
OWN = 17
WINDOW = 42


def cubic_weights(fraction):
    position = 1.0 - jnp.full((8, 128), fraction, jnp.float32)
    taps = (
        -position * (position - 1.0) * (position - 2.0) / 6.0,
        (position + 1.0) * (position - 1.0) * (position - 2.0) / 2.0,
        -(position + 1.0) * position * (position - 2.0) / 2.0,
        (position + 1.0) * position * (position - 1.0) / 6.0,
    )
    return taps[::-1]


def kernel(
    fine_hbm,
    coarse_hbm,
    upstream_x_hbm,
    upstream_y_hbm,
    fractions_hbm,
    out_ref,
    fine_ref,
    coarse_ref,
    upstream_x,
    upstream_y,
    fractions,
    packed_f,
    slabs_c,
    chosen_c,
    pencil_c,
    cells,
    edges,
    ahead,
    fringe,
    window_1,
    ready,
    strewn,
    swept_0,
    rows,
    swept_2,
    back_f,
    back_c,
    sent,
    got,
    brought,
):
    arrivals = [
        pltpu.make_async_copy(source, target, brought.at[i])
        for i, (source, target) in enumerate(
            (
                (fine_hbm, fine_ref),
                (upstream_x_hbm, upstream_x),
                (upstream_y_hbm, upstream_y),
                (fractions_hbm, fractions),
                (coarse_hbm, coarse_ref),
            )
        )
    ]
    for arrival in arrivals:
        arrival.start()
    gx, gy = lax.axis_index("gx"), lax.axis_index("gy")
    plane, member = gx // GROUP, lax.rem(gx, GROUP)
    parity = lax.rem(gy, 2)

    def quarter_of(other, odd):
        along = lax.rem(other, 4)
        return along + odd * (1 - 2 * lax.rem(along, 2))

    quarter, level = quarter_of(member, parity), member // 4
    lane = lax.broadcasted_iota(jnp.int32, (8, 128), 1)
    low = lane < HALF
    within = lax.rem(lane, HALF)

    def in_plane(other, gy_step=0):
        return plane * GROUP + other, lax.rem(gy + gy_step + RING, RING)

    def up_planes(step):
        return lax.rem(plane + step + PLANES, PLANES) * GROUP + member, gy

    def mate(step):
        return lax.rem(member + step, GROUP)

    def swap(tile):
        return pltpu.roll(tile, HALF, 1)

    def remote(source, target, channel, device, leave=None):
        leave = channel if leave is None else leave
        return pltpu.make_async_remote_copy(
            source, target, sent.at[leave], got.at[channel], device_id=device, device_id_type=MESH
        )

    def drain(ref, semaphores, channel):
        pltpu.make_async_copy(ref, ref, semaphores.at[channel]).wait()

    barrier = pltpu.get_barrier_semaphore()

    def greet(device):
        pl.semaphore_signal(barrier, inc=1, device_id=device, device_id_type=MESH)

    edge = jnp.logical_or(quarter == 0, quarter == 3)
    outer = jnp.logical_or(member == 0, member == GROUP - 1)
    outward = jnp.where(quarter == 0, -1, 1)
    for step in (3, -3, 2, -2, 1, -1):
        greet(up_planes(step))

    @pl.when(edge)
    def _():
        for other in range(GROUP):
            greet(in_plane(other, outward))

    for step in range(1, GROUP):
        greet(in_plane(mate(step)))

    def pack(field, place):
        for lev in range(2):
            for block in range(2):
                columns = slice(128 * block, 128 * block + 128)
                upper = field[lev, 0:8, columns]
                lower = field[lev, 8:16, columns]
                place(lev, 2 * block, jnp.where(low, upper, swap(lower)))
                place(lev, 2 * block + 1, jnp.where(low, swap(upper), lower))

    def planes_start(slabs, channel):
        own = slabs.at[3]

        @pl.when(member == GROUP - 1)
        def _():
            remote(own, slabs.at[0], channel, up_planes(3), channel + 4).start()

        @pl.when(member == 0)
        def _():
            remote(own, slabs.at[6], channel, up_planes(-3), channel + 4).start()

        for step in (2, -2, 1, -1):
            remote(own, slabs.at[3 - step], channel, up_planes(step)).start()

    def planes_wait(slabs, channel):
        @pl.when(outer)
        def _():
            drain(slabs.at[pl.ds(0, 5)], got, channel)

        @pl.when(jnp.logical_not(outer))
        def _():
            drain(slabs.at[pl.ds(0, 4)], got, channel)

    def choose(slabs, chosen, pass_row):
        for block in range(2):
            first = (upstream_x[pass_row, 2 * gy + block] - 1 + 16 * OWN) // 16
            slab = (first + lax.rem(member + 1 - first + 48, GROUP) + 7) // 8
            later = jnp.minimum(slab + 1, 6)
            for lev in range(2):
                for half in range(2):
                    tile = 4 * lev + 2 * block + half
                    chosen[tile, 0] = slabs[slab, tile]
                    chosen[tile, 1] = slabs[later, tile]

    def transpose_start(chosen, pencil, channel):
        for step in range(1, GROUP):
            other = mate(step)
            tile = 4 * (other // 4) + quarter_of(other, parity)
            remote(chosen.at[tile], pencil.at[member], channel, in_plane(other)).start()
        pencil[member] = chosen[4 * level + quarter]

    def transpose_wait(pencil, channel):
        drain(pencil.at[pl.ds(0, 7)], got, channel)

    def sweep_x(load, pass_row, block):
        shift = upstream_x[pass_row, block]
        weights = cubic_weights(fractions[0, pass_row])
        start = shift - 1 + 16 * OWN
        first = start // 16
        return slide([load(first, i) for i in range(10)], start, weights)

    def slide(even_tiles, start, weights):
        count = len(even_tiles) - 2
        odd, inner = lax.rem(start // 8, 2), lax.rem(start, 8)
        swapped = [swap(tile) for tile in even_tiles]
        odd_tiles = [jnp.where(low, swapped[i], swapped[i + 1]) for i in range(count + 1)]
        is_odd = jnp.full((8, 128), odd, jnp.int32) == 1
        lead = [jnp.where(is_odd, odd_tiles[i], even_tiles[i]) for i in range(count + 1)]
        for i in range(count):
            rows[i, 0:8] = lead[i]
            rows[i, 8:16] = jnp.where(is_odd, even_tiles[i + 1], odd_tiles[i])
            rows[i, 16:24] = lead[i + 1]
        sums = []
        for i in range(count):
            summed = weights[0] * rows[i, pl.ds(inner, 8)]
            for tap in range(1, 4):
                summed = summed + weights[tap] * rows[i, pl.ds(inner + tap, 8)]
            sums.append(summed)
        return sums

    def shifted_cells(load, i, offset):
        side = (offset >= 0).astype(jnp.int32)
        turn = offset + HALF * (1 - side)
        return jnp.where(
            within + turn < HALF,
            pltpu.roll(load(i, side), lax.rem(128 - turn, 128), 1),
            pltpu.roll(load(i, side + 1), HALF - turn, 1),
        )

    border = HALF * lax.rem(quarter, 2)
    low_block = lax.rem(2 * gy + (quarter + 1) // 2 - 1 + 2 * RING, 2 * RING)
    high_block = lax.rem(low_block + 1, 2 * RING)

    def crossing_of(to_plane):
        return border - upstream_y[1, to_plane] - 2

    def sweep_y_ahead(to_plane, tiles, target, at):
        shift = upstream_y[1, to_plane]
        crossing = crossing_of(to_plane)
        upper_columns = within > crossing + 2
        spare = jnp.zeros((8, 128), jnp.float32)
        parts = []
        for tap, weight in enumerate(cubic_weights(fractions[1, 1])):
            offset = shift - 1 + tap
            split = jnp.logical_and(within + offset >= border, jnp.logical_not(upper_columns))
            parts.append((offset, jnp.where(split, 0.0, weight), jnp.where(split, weight, 0.0)))
        for n, i in enumerate(tiles):
            main = jnp.zeros((8, 128), jnp.float32)
            second = jnp.zeros((8, 128), jnp.float32)
            for offset, first_weight, second_weight in parts:
                moved = shifted_cells(lambda i, side: cells[i, side], i, offset)
                main = main + first_weight * moved
                second = second + second_weight * moved
            target[at + n] = main
            spare = spare + pltpu.roll(second, lax.rem(8 * i - crossing + 256, 128), 1)
        target[at + len(tiles)] = spare

    def sweep_x_both():
        crossing = crossing_of(plane)
        upper_columns = within > crossing + 2
        both = jnp.logical_and(within >= crossing, within <= crossing + 2)

        def load_low(first, i):
            i = first + i
            place = 9 * ((i + 7) // 8) + lax.rem(i + 7, 8)
            return jnp.where(upper_columns, 0.0, window_1[place])

        def load_high(first, i):
            i = first + i
            level_plane, inside = (i + 7) // 8, lax.rem(i + 7, 8)
            spare = window_1[jnp.where(level_plane == 6, 55, 9 * level_plane + 8)]
            spare = pltpu.roll(spare, lax.rem(crossing - 8 * inside + 256, 128), 1)
            return jnp.where(upper_columns, window_1[9 * level_plane + inside], jnp.where(both, spare, 0.0))

        low_part = sweep_x(load_low, 1, low_block)
        high_part = sweep_x(load_high, 1, high_block)
        return [a + b for a, b in zip(low_part, high_part)]

    def sweep_y(pass_row, load, count):
        shift = upstream_y[pass_row, plane]
        weights = cubic_weights(fractions[1, pass_row])
        sums = [None] * count
        for tap in range(4):
            for i in range(count):
                term = weights[tap] * shifted_cells(load, i, shift - 1 + tap)
                sums[i] = term if sums[i] is None else sums[i] + term
        return sums

    def back_start(swept, back, channel):
        for step in range(1, GROUP):
            other = mate(step)
            remote(swept.at[other], back.at[level, quarter + 1], channel, in_plane(other)).start()
        back[level, quarter + 1] = swept[member]

        @pl.when(edge)
        def _():
            side = jnp.where(quarter == 0, 5, 0)
            for other in range(GROUP):
                remote(swept.at[other], back.at[level, side], channel, in_plane(other, outward), channel + 2).start()

    def back_wait(channel):
        drain(strewn.at[pl.ds(0, 11)], got, channel)

    blank = jnp.zeros((8, 128), jnp.float32)
    for i in (0, 1, 10, 11):
        ready[i] = blank
    for i in range(76):
        strewn[i] = blank

    @pl.when(jnp.logical_and(member > 0, member < 7))
    def _():
        for lev in range(2):
            for part in range(6):
                back_f[lev, part, 5] = blank

    def place_f(lev, part, tile):
        packed_f[lev, part + 1] = tile

    def place_c(lev, part, tile):
        slabs_c[3, 4 * lev + part] = tile

    for lev in range(2):
        packed_f[lev, 0] = jnp.zeros((8, 128), jnp.float32)
        packed_f[lev, 5] = jnp.zeros((8, 128), jnp.float32)
    arrivals[0].wait()
    pack(fine_ref, place_f)
    pl.semaphore_wait(barrier, 17)

    for lev in range(2):
        remote(packed_f.at[lev, 4], edges.at[member], 3, in_plane(4 * lev + 1 - parity, 1)).start()
        remote(packed_f.at[lev, 1], edges.at[member], 3, in_plane(4 * lev + 2 + parity, -1)).start()
    for step in range(1, GROUP):
        other = mate(step)
        source = packed_f.at[other // 4, pl.ds(quarter_of(other, parity), 3)]
        remote(source, cells.at[member], 0, in_plane(other)).start()
    cells[member] = packed_f[level, pl.ds(quarter, 3)]
    arrivals[4].wait()
    pack(coarse_ref, place_c)
    planes_start(slabs_c, 1)
    for arrival in arrivals[1:4]:
        arrival.wait()
    drain(cells.at[pl.ds(0, 7)], got, 0)

    @pl.when(edge)
    def _():
        drain(edges, got, 3)
        side = jnp.where(quarter == 0, 0, 2)
        for i in range(8):
            cells[i, side] = edges[i]

    def to(step):
        return lax.rem(plane + step + PLANES, PLANES)

    sweep_y_ahead(to(3), (7,), fringe, 0)
    remote(fringe.at[pl.ds(0, 2)], window_1.at[pl.ds(7, 2)], 2, up_planes(3)).start()
    sweep_y_ahead(to(-3), (0,), fringe, 2)
    remote(fringe.at[pl.ds(2, 2)], window_1.at[pl.ds(54, 2)], 2, up_planes(-3)).start()
    for n, step in enumerate((2, -2, 1, -1)):
        sweep_y_ahead(to(step), range(8), ahead, 9 * n)
        target = window_1.at[pl.ds(9 * (3 - step), 9)]
        remote(ahead.at[pl.ds(9 * n, 9)], target, 2, up_planes(step)).start()
    sweep_y_ahead(plane, range(8), window_1, 27)
    planes_wait(slabs_c, 1)
    choose(slabs_c, chosen_c, 2)
    transpose_start(chosen_c, pencil_c, 4)
    own_block = 2 * gy + quarter // 2
    transpose_wait(pencil_c, 4)
    coarse_rows = sweep_x(lambda first, i: pencil_c[lax.rem(first + i + 7, 8), i // 8], 2, own_block)
    for i, tile in enumerate(coarse_rows):
        swept_2[i] = tile
    back_start(swept_2, back_c, 6)

    drain(window_1.at[pl.ds(0, 40)], got, 2)

    for i, tile in enumerate(sweep_x_both()):
        ready[2 + i] = tile
    start = upstream_x[0, own_block] - 1 + 16 * OWN
    parts = slide([ready[i] for i in range(12)], start, cubic_weights(fractions[0, 0]))
    for i, tile in enumerate(parts):
        strewn[32 + i] = tile
    for i in range(WINDOW):
        swept_0[i] = strewn[start // 16 + i]

    def scatter_start(step, others, slot, outer_gy):
        def start_at(gy_step, side, leave, skip):
            for other in others:
                target_plane = lax.rem(plane - step + PLANES, PLANES)
                copy = remote(
                    swept_0.at[OWN - 8 * step + other],
                    back_f.at[level, side, slot],
                    7,
                    (target_plane * GROUP + other, lax.rem(gy + gy_step + RING, RING)),
                    leave,
                )
                if skip:
                    pl.when(other != member)(copy.start)
                else:
                    copy.start()

        if outer_gy:
            @pl.when(edge)
            def _():
                start_at(outward, jnp.where(quarter == 0, 5, 0), 9, False)
        else:
            start_at(0, quarter + 1, 7, step == 0)

    for outer_gy in (True, False):
        scatter_start(3, (7,), 5, outer_gy)
        scatter_start(-3, (0,), 5, outer_gy)
        for step in (2, -2, 1, -1, 0):
            scatter_start(step, range(GROUP), step + 2, outer_gy)
    back_f[level, quarter + 1, 2] = swept_0[OWN + member]

    back_wait(6)
    coarse = sweep_y(2, lambda i, side: back_c[i // 4, lax.rem(i, 4) + side], 8)

    @pl.when(outer)
    def _():
        drain(strewn.at[pl.ds(0, 71)], got, 7)

    @pl.when(jnp.logical_not(outer))
    def _():
        drain(strewn.at[pl.ds(0, 59)], got, 7)

    for lev in range(2):
        for part in range(6):
            total = back_f[lev, part, 0]
            for slot in range(1, 6):
                total = total + back_f[lev, part, slot]
            ready[lev * 6 + part] = total
    fine = sweep_y(0, lambda i, side: ready[6 * (i // 4) + lax.rem(i, 4) + side], 8)
    tiles = [a - b for a, b in zip(fine, coarse)]
    for lev in range(2):
        for block in range(2):
            columns = slice(128 * block, 128 * block + 128)
            even, odd = tiles[lev * 4 + 2 * block], tiles[lev * 4 + 2 * block + 1]
            out_ref[lev, 0:8, columns] = jnp.where(low, even, swap(odd))
            out_ref[lev, 8:16, columns] = jnp.where(low, swap(even), odd)

    drain(cells.at[pl.ds(0, 7)], sent, 0)
    drain(slabs_c.at[pl.ds(0, 4)], sent, 1)

    @pl.when(outer)
    def _():
        drain(slabs_c.at[0], sent, 5)

    drain(strewn.at[pl.ds(0, 4)], sent, 3)
    drain(window_1.at[pl.ds(0, 40)], sent, 2)
    drain(pencil_c.at[pl.ds(0, 7)], sent, 4)
    drain(strewn.at[pl.ds(0, 7)], sent, 6)
    drain(strewn.at[pl.ds(0, 41)], sent, 7)

    @pl.when(edge)
    def _():
        drain(strewn.at[pl.ds(0, 8)], sent, 8)
        drain(strewn.at[pl.ds(0, 42)], sent, 9)


def local(fine_cotangent, coarse_cotangent, upstream_x, upstream_y, fractions):
    vmem = pl.BlockSpec(memory_space=pltpu.VMEM)
    anywhere = pl.BlockSpec(memory_space=pl.ANY)

    def tiles(*shape):
        return pltpu.VMEM((*shape, 8, 128), jnp.float32)

    return pl.pallas_call(
        kernel,
        out_shape=pltpu.VMEM(fine_cotangent.shape, jnp.float32),
        in_specs=[anywhere] * 5,
        out_specs=vmem,
        scratch_shapes=[
            pltpu.VMEM(fine_cotangent.shape, jnp.float32),
            pltpu.VMEM(fine_cotangent.shape, jnp.float32),
            pltpu.SMEM(upstream_x.shape, jnp.int32),
            pltpu.SMEM(upstream_y.shape, jnp.int32),
            pltpu.SMEM((2, 3), jnp.float32),
            tiles(2, 6),
            tiles(7, 8),
            tiles(8, 2),
            tiles(8, 2),
            tiles(8, 3),
            tiles(8),
            tiles(36),
            tiles(4),
            tiles(63),
            tiles(12),
            tiles(76),
            tiles(WINDOW),
            pltpu.VMEM((10, 24, 128), jnp.float32),
            tiles(8),
            tiles(2, 6, 6),
            tiles(2, 6),
            pltpu.SemaphoreType.DMA((10,)),
            pltpu.SemaphoreType.DMA((8,)),
            pltpu.SemaphoreType.DMA((5,)),
        ],
        compiler_params=pltpu.CompilerParams(collective_id=0, has_side_effects=True),
    )(fine_cotangent, coarse_cotangent, upstream_x, upstream_y, fractions.T)


def solution(mesh):
    placed = (P(None, "gx", "gy"), P(None, "gx", "gy"), P(), P(), P())
    return jax.shard_map(
        local, mesh=mesh, in_specs=placed, out_specs=P(None, "gx", "gy"), check_vma=False
    )
```

```python
import jax
import jax.numpy as jnp
from jax import lax
from jax.experimental import pallas as pl
from jax.experimental.pallas import tpu as pltpu
from jax.sharding import PartitionSpec as P

MESH = pl.DeviceIdType.MESH
PLANES = 16
GROUP = 8
RING = 4
HALF = 64
OWN = 17
WINDOW = 42


def cubic_weights(fraction):
    position = 1.0 - jnp.full((8, 128), fraction, jnp.float32)
    taps = (
        -position * (position - 1.0) * (position - 2.0) / 6.0,
        (position + 1.0) * (position - 1.0) * (position - 2.0) / 2.0,
        -(position + 1.0) * position * (position - 2.0) / 2.0,
        (position + 1.0) * position * (position - 1.0) / 6.0,
    )
    return taps[::-1]


def kernel(
    fine_hbm,
    coarse_hbm,
    upstream_x_hbm,
    upstream_y_hbm,
    fractions_hbm,
    out_ref,
    fine_ref,
    coarse_ref,
    upstream_x,
    upstream_y,
    fractions,
    packed_f,
    slabs_c,
    chosen_c,
    pencil_c,
    cells,
    mixed,
    edges,
    ahead,
    fringe,
    window_1,
    taps,
    ready,
    strewn,
    swept_0,
    rows,
    rows_high,
    swept_2,
    back_f,
    back_c,
    sent,
    got,
    brought,
):
    arrivals = [
        pltpu.make_async_copy(source, target, brought.at[i])
        for i, (source, target) in enumerate(
            (
                (fine_hbm, fine_ref),
                (upstream_x_hbm, upstream_x),
                (upstream_y_hbm, upstream_y),
                (fractions_hbm, fractions),
                (coarse_hbm, coarse_ref),
            )
        )
    ]
    arrivals[0].start()
    gx, gy = lax.axis_index("gx"), lax.axis_index("gy")
    plane, member = gx // GROUP, lax.rem(gx, GROUP)
    parity = lax.rem(gy, 2)

    def quarter_of(other, odd):
        along = lax.rem(other, 4)
        return along + odd * (1 - 2 * lax.rem(along, 2))

    quarter, level = quarter_of(member, parity), member // 4
    lane = lax.broadcasted_iota(jnp.int32, (8, 128), 1)
    low = lane < HALF
    within = lax.rem(lane, HALF)

    def in_plane(other, gy_step=0):
        return plane * GROUP + other, lax.rem(gy + gy_step + RING, RING)

    def up_planes(step):
        return lax.rem(plane + step + PLANES, PLANES) * GROUP + member, gy

    def mate(step):
        return lax.rem(member + step, GROUP)

    def swap(tile):
        return pltpu.roll(tile, HALF, 1)

    def remote(source, target, channel, device, leave=None):
        leave = channel if leave is None else leave
        return pltpu.make_async_remote_copy(
            source, target, sent.at[leave], got.at[channel], device_id=device, device_id_type=MESH
        )

    def drain(ref, semaphores, channel):
        pltpu.make_async_copy(ref, ref, semaphores.at[channel]).wait()

    barrier = pltpu.get_barrier_semaphore()

    def greet(device):
        pl.semaphore_signal(barrier, inc=1, device_id=device, device_id_type=MESH)

    edge = jnp.logical_or(quarter == 0, quarter == 3)
    outer = jnp.logical_or(member == 0, member == GROUP - 1)
    outward = jnp.where(quarter == 0, -1, 1)
    for step in (3, -3, 2, -2, 1, -1):
        greet(up_planes(step))

    @pl.when(edge)
    def _():
        for other in range(GROUP):
            greet(in_plane(other, outward))

    for step in range(1, GROUP):
        greet(in_plane(mate(step)))
    for arrival in arrivals[1:]:
        arrival.start()

    def pack(field, place):
        for lev in range(2):
            for block in range(2):
                columns = slice(128 * block, 128 * block + 128)
                upper = field[lev, 0:8, columns]
                lower = field[lev, 8:16, columns]
                place(lev, 2 * block, jnp.where(low, upper, swap(lower)))
                place(lev, 2 * block + 1, jnp.where(low, swap(upper), lower))

    def weights_of(pass_row, direction):
        return [taps[2 * pass_row + direction, tap] for tap in range(4)]

    def planes_start(slabs, channel):
        own = slabs.at[3]

        @pl.when(member == GROUP - 1)
        def _():
            remote(own, slabs.at[0], channel, up_planes(3), channel + 4).start()

        @pl.when(member == 0)
        def _():
            remote(own, slabs.at[6], channel, up_planes(-3), channel + 4).start()

        for step in (2, -2, 1, -1):
            remote(own, slabs.at[3 - step], channel, up_planes(step)).start()

    def planes_wait(slabs, channel):
        @pl.when(outer)
        def _():
            drain(slabs.at[pl.ds(0, 5)], got, channel)

        @pl.when(jnp.logical_not(outer))
        def _():
            drain(slabs.at[pl.ds(0, 4)], got, channel)

    def choose(slabs, chosen, pass_row):
        for block in range(2):
            first = (upstream_x[pass_row, 2 * gy + block] - 1 + 16 * OWN) // 16
            slab = (first + lax.rem(member + 1 - first + 48, GROUP) + 7) // 8
            later = jnp.minimum(slab + 1, 6)
            for lev in range(2):
                for half in range(2):
                    tile = 4 * lev + 2 * block + half
                    chosen[tile, 0] = slabs[slab, tile]
                    chosen[tile, 1] = slabs[later, tile]

    def transpose_start(chosen, pencil, channel):
        for step in range(1, GROUP):
            other = mate(step)
            tile = 4 * (other // 4) + quarter_of(other, parity)
            remote(chosen.at[tile], pencil.at[member], channel, in_plane(other)).start()
        pencil[member] = chosen[4 * level + quarter]

    def transpose_wait(pencil, channel):
        drain(pencil.at[pl.ds(0, 7)], got, channel)

    def sweep_x(load, pass_row, block, rows=rows):
        shift = upstream_x[pass_row, block]
        weights = weights_of(pass_row, 0)
        start = shift - 1 + 16 * OWN
        first = start // 16
        return slide([load(first, i) for i in range(10)], start, weights, rows)

    def slide(even_tiles, start, weights, rows=rows):
        count = len(even_tiles) - 2
        odd, inner = lax.rem(start // 8, 2), lax.rem(start, 8)
        swapped = [swap(tile) for tile in even_tiles]
        odd_tiles = [jnp.where(low, swapped[i], swapped[i + 1]) for i in range(count + 1)]
        is_odd = jnp.full((8, 128), odd, jnp.int32) == 1
        lead = [jnp.where(is_odd, odd_tiles[i], even_tiles[i]) for i in range(count + 1)]
        for i in range(count):
            rows[i, 0:8] = lead[i]
            rows[i, 8:16] = jnp.where(is_odd, even_tiles[i + 1], odd_tiles[i])
            rows[i, 16:24] = lead[i + 1]
        sums = []
        for i in range(count):
            summed = weights[0] * rows[i, pl.ds(inner, 8)]
            for tap in range(1, 4):
                summed = summed + weights[tap] * rows[i, pl.ds(inner + tap, 8)]
            sums.append(summed)
        return sums

    def shifted_cells(load, i, offset):
        side = (offset >= 0).astype(jnp.int32)
        turn = offset + HALF * (1 - side)
        return jnp.where(
            within + turn < HALF,
            pltpu.roll(load(i, side), lax.rem(128 - turn, 128), 1),
            pltpu.roll(load(i, side + 1), HALF - turn, 1),
        )

    border = HALF * lax.rem(quarter, 2)
    low_block = lax.rem(2 * gy + (quarter + 1) // 2 - 1 + 2 * RING, 2 * RING)
    high_block = lax.rem(low_block + 1, 2 * RING)

    def crossing_of(to_plane):
        return border - upstream_y[1, to_plane] - 2

    def mix_ahead():
        weights = weights_of(1, 1)
        blank_tile = jnp.zeros((8, 128), jnp.float32)
        kept, split_off = {}, {}
        for side in range(2):
            for tap in range(1, 4):
                split = jnp.logical_and(within + tap >= HALF, lax.rem(quarter, 2) == side)
                kept[side, tap] = jnp.where(split, 0.0, weights[tap])
                split_off[side, tap] = jnp.where(split, weights[tap], 0.0)
        spare = blank_tile
        for i in range(8):
            second = blank_tile
            for side in range(3):
                main = weights[0] * cells[i, side]
                for tap in range(1, 4):
                    moved = pltpu.roll(cells[i, side], 128 - tap, 1)
                    if side == 2:
                        main = main + weights[tap] * moved
                        continue
                    moved = jnp.where(within + tap < HALF, moved, pltpu.roll(cells[i, side + 1], HALF - tap, 1))
                    main = main + kept[side, tap] * moved
                    second = second + split_off[side, tap] * moved
                mixed[i, side] = main
            spare = spare + pltpu.roll(second, (8 * i - 61) % 128, 1)
        return spare

    def sweep_y_ahead(to_plane, tiles, target, at):
        offset = upstream_y[1, to_plane] - 1
        for n, i in enumerate(tiles):
            target[at + n] = shifted_cells(lambda i, side: mixed[i, side], i, offset)
        target[at + len(tiles)] = spare

    def sweep_x_both():
        crossing = crossing_of(plane)
        upper_columns = within > crossing + 2
        both = jnp.logical_and(within >= crossing, within <= crossing + 2)

        def load_low(first, i):
            i = first + i
            place = 9 * ((i + 7) // 8) + lax.rem(i + 7, 8)
            return jnp.where(upper_columns, 0.0, window_1[place])

        def load_high(first, i):
            i = first + i
            level_plane, inside = (i + 7) // 8, lax.rem(i + 7, 8)
            spare = window_1[jnp.where(level_plane == 6, 55, 9 * level_plane + 8)]
            spare = pltpu.roll(spare, lax.rem(crossing - 8 * inside + 256, 128), 1)
            return jnp.where(upper_columns, window_1[9 * level_plane + inside], jnp.where(both, spare, 0.0))

        low_part = sweep_x(load_low, 1, low_block)
        high_part = sweep_x(load_high, 1, high_block, rows_high)
        return [a + b for a, b in zip(low_part, high_part)]

    def sweep_y(pass_row, load, count):
        shift = upstream_y[pass_row, plane]
        weights = weights_of(pass_row, 1)
        sums = [None] * count
        for tap in range(4):
            for i in range(count):
                term = weights[tap] * shifted_cells(load, i, shift - 1 + tap)
                sums[i] = term if sums[i] is None else sums[i] + term
        return sums

    def back_start(swept, back, channel):
        for step in range(1, GROUP):
            other = mate(step)
            remote(swept.at[other], back.at[level, quarter + 1], channel, in_plane(other)).start()
        back[level, quarter + 1] = swept[member]

        @pl.when(edge)
        def _():
            side = jnp.where(quarter == 0, 5, 0)
            for other in range(GROUP):
                remote(swept.at[other], back.at[level, side], channel, in_plane(other, outward), channel + 2).start()

    def back_wait(channel):
        drain(strewn.at[pl.ds(0, 11)], got, channel)

    blank = jnp.zeros((8, 128), jnp.float32)
    for i in (0, 1, 10, 11):
        ready[i] = blank
    for i in range(76):
        strewn[i] = blank

    @pl.when(jnp.logical_and(member > 0, member < 7))
    def _():
        for lev in range(2):
            for part in range(6):
                back_f[lev, part, 5] = blank

    def place_f(lev, part, tile):
        packed_f[lev, part + 1] = tile

    def place_c(lev, part, tile):
        slabs_c[3, 4 * lev + part] = tile

    for lev in range(2):
        packed_f[lev, 0] = jnp.zeros((8, 128), jnp.float32)
        packed_f[lev, 5] = jnp.zeros((8, 128), jnp.float32)
    arrivals[0].wait()
    pack(fine_ref, place_f)
    pl.semaphore_wait(barrier, 17)

    for lev in range(2):
        remote(packed_f.at[lev, 4], edges.at[member], 3, in_plane(4 * lev + 1 - parity, 1)).start()
        remote(packed_f.at[lev, 1], edges.at[member], 3, in_plane(4 * lev + 2 + parity, -1)).start()
    for step in range(1, GROUP):
        other = mate(step)
        source = packed_f.at[other // 4, pl.ds(quarter_of(other, parity), 3)]
        remote(source, cells.at[member], 0, in_plane(other)).start()
    cells[member] = packed_f[level, pl.ds(quarter, 3)]
    arrivals[4].wait()
    pack(coarse_ref, place_c)
    planes_start(slabs_c, 1)
    for arrival in arrivals[1:4]:
        arrival.wait()
    for pass_row in range(3):
        for direction in range(2):
            for tap, weight in enumerate(cubic_weights(fractions[direction, pass_row])):
                taps[2 * pass_row + direction, tap] = weight
    drain(cells.at[pl.ds(0, 7)], got, 0)

    @pl.when(edge)
    def _():
        drain(edges, got, 3)
        side = jnp.where(quarter == 0, 0, 2)
        for i in range(8):
            cells[i, side] = edges[i]

    def to(step):
        return lax.rem(plane + step + PLANES, PLANES)

    spare = mix_ahead()
    sweep_y_ahead(to(3), (7,), fringe, 0)
    remote(fringe.at[pl.ds(0, 2)], window_1.at[pl.ds(7, 2)], 2, up_planes(3)).start()
    sweep_y_ahead(to(-3), (0,), fringe, 2)
    remote(fringe.at[pl.ds(2, 2)], window_1.at[pl.ds(54, 2)], 2, up_planes(-3)).start()
    for n, step in enumerate((2, -2, 1, -1)):
        sweep_y_ahead(to(step), range(8), ahead, 9 * n)
        target = window_1.at[pl.ds(9 * (3 - step), 9)]
        remote(ahead.at[pl.ds(9 * n, 9)], target, 2, up_planes(step)).start()
    sweep_y_ahead(plane, range(8), window_1, 27)
    planes_wait(slabs_c, 1)
    choose(slabs_c, chosen_c, 2)
    transpose_start(chosen_c, pencil_c, 4)
    own_block = 2 * gy + quarter // 2
    transpose_wait(pencil_c, 4)
    coarse_rows = sweep_x(lambda first, i: pencil_c[lax.rem(first + i + 7, 8), i // 8], 2, own_block)
    for i, tile in enumerate(coarse_rows):
        swept_2[i] = tile
    back_start(swept_2, back_c, 6)

    drain(window_1.at[pl.ds(0, 40)], got, 2)

    for i, tile in enumerate(sweep_x_both()):
        ready[2 + i] = tile
    start = upstream_x[0, own_block] - 1 + 16 * OWN
    parts = slide([ready[i] for i in range(12)], start, weights_of(0, 0))
    for i, tile in enumerate(parts):
        strewn[32 + i] = tile
    for i in range(WINDOW):
        swept_0[i] = strewn[start // 16 + i]

    def scatter_start(step, others, slot, outer_gy):
        def start_at(gy_step, side, leave, skip):
            for other in others:
                target_plane = lax.rem(plane - step + PLANES, PLANES)
                copy = remote(
                    swept_0.at[OWN - 8 * step + other],
                    back_f.at[level, side, slot],
                    7,
                    (target_plane * GROUP + other, lax.rem(gy + gy_step + RING, RING)),
                    leave,
                )
                if skip:
                    pl.when(other != member)(copy.start)
                else:
                    copy.start()

        if outer_gy:
            @pl.when(edge)
            def _():
                start_at(outward, jnp.where(quarter == 0, 5, 0), 9, False)
        else:
            start_at(0, quarter + 1, 7, step == 0)

    for outer_gy in (True, False):
        scatter_start(3, (7,), 5, outer_gy)
        scatter_start(-3, (0,), 5, outer_gy)
    for outer_gy in (True, False):
        for step in (2, -2, 1, -1, 0):
            scatter_start(step, range(GROUP), step + 2, outer_gy)
    back_f[level, quarter + 1, 2] = swept_0[OWN + member]

    back_wait(6)
    coarse = sweep_y(2, lambda i, side: back_c[i // 4, lax.rem(i, 4) + side], 8)

    drain(cells.at[pl.ds(0, 7)], sent, 0)
    drain(slabs_c.at[pl.ds(0, 4)], sent, 1)

    @pl.when(outer)
    def _():
        drain(slabs_c.at[0], sent, 5)

    drain(strewn.at[pl.ds(0, 4)], sent, 3)
    drain(window_1.at[pl.ds(0, 40)], sent, 2)
    drain(pencil_c.at[pl.ds(0, 7)], sent, 4)
    drain(strewn.at[pl.ds(0, 7)], sent, 6)
    drain(strewn.at[pl.ds(0, 41)], sent, 7)

    @pl.when(edge)
    def _():
        drain(strewn.at[pl.ds(0, 8)], sent, 8)
        drain(strewn.at[pl.ds(0, 42)], sent, 9)

    @pl.when(outer)
    def _():
        drain(strewn.at[pl.ds(0, 71)], got, 7)

    @pl.when(jnp.logical_not(outer))
    def _():
        drain(strewn.at[pl.ds(0, 59)], got, 7)

    for lev in range(2):
        for part in range(6):
            total = back_f[lev, part, 0]
            for slot in range(1, 6):
                total = total + back_f[lev, part, slot]
            ready[lev * 6 + part] = total
    fine = sweep_y(0, lambda i, side: ready[6 * (i // 4) + lax.rem(i, 4) + side], 8)
    tiles = [a - b for a, b in zip(fine, coarse)]
    for lev in range(2):
        for block in range(2):
            columns = slice(128 * block, 128 * block + 128)
            even, odd = tiles[lev * 4 + 2 * block], tiles[lev * 4 + 2 * block + 1]
            out_ref[lev, 0:8, columns] = jnp.where(low, even, swap(odd))
            out_ref[lev, 8:16, columns] = jnp.where(low, swap(even), odd)


def local(fine_cotangent, coarse_cotangent, upstream_x, upstream_y, fractions):
    vmem = pl.BlockSpec(memory_space=pltpu.VMEM)
    anywhere = pl.BlockSpec(memory_space=pl.ANY)

    def tiles(*shape):
        return pltpu.VMEM((*shape, 8, 128), jnp.float32)

    return pl.pallas_call(
        kernel,
        out_shape=pltpu.VMEM(fine_cotangent.shape, jnp.float32),
        in_specs=[anywhere] * 5,
        out_specs=vmem,
        scratch_shapes=[
            pltpu.VMEM(fine_cotangent.shape, jnp.float32),
            pltpu.VMEM(fine_cotangent.shape, jnp.float32),
            pltpu.SMEM(upstream_x.shape, jnp.int32),
            pltpu.SMEM(upstream_y.shape, jnp.int32),
            pltpu.SMEM((2, 3), jnp.float32),
            tiles(2, 6),
            tiles(7, 8),
            tiles(8, 2),
            tiles(8, 2),
            tiles(8, 3),
            tiles(8, 3),
            tiles(8),
            tiles(36),
            tiles(4),
            tiles(63),
            tiles(6, 4),
            tiles(12),
            tiles(76),
            tiles(WINDOW),
            pltpu.VMEM((10, 24, 128), jnp.float32),
            pltpu.VMEM((10, 24, 128), jnp.float32),
            tiles(8),
            tiles(2, 6, 6),
            tiles(2, 6),
            pltpu.SemaphoreType.DMA((10,)),
            pltpu.SemaphoreType.DMA((8,)),
            pltpu.SemaphoreType.DMA((5,)),
        ],
        compiler_params=pltpu.CompilerParams(collective_id=0, has_side_effects=True),
    )(fine_cotangent, coarse_cotangent, upstream_x, upstream_y, fractions.T)


def solution(mesh):
    placed = (P(None, "gx", "gy"), P(None, "gx", "gy"), P(), P(), P())
    return jax.shard_map(
        local, mesh=mesh, in_specs=placed, out_specs=P(None, "gx", "gy"), check_vma=False
    )
```

```python
import jax
import jax.numpy as jnp
from jax import lax
from jax.experimental import pallas as pl
from jax.experimental.pallas import tpu as pltpu
from jax.sharding import PartitionSpec as P

MESH = pl.DeviceIdType.MESH
PLANES = 16
GROUP = 8
RING = 4
HALF = 64
OWN = 17
WINDOW = 42


def cubic_weights(fraction):
    position = 1.0 - jnp.full((8, 128), fraction, jnp.float32)
    taps = (
        -position * (position - 1.0) * (position - 2.0) / 6.0,
        (position + 1.0) * (position - 1.0) * (position - 2.0) / 2.0,
        -(position + 1.0) * position * (position - 2.0) / 2.0,
        (position + 1.0) * position * (position - 1.0) / 6.0,
    )
    return taps[::-1]


def kernel(
    fine_hbm,
    coarse_hbm,
    upstream_x_hbm,
    upstream_y_hbm,
    fractions_hbm,
    out_ref,
    fine_ref,
    coarse_ref,
    upstream_x,
    upstream_y,
    fractions,
    packed_f,
    slabs_c,
    chosen_c,
    pencil_c,
    cells,
    mixed,
    edges,
    ahead,
    fringe,
    window_1,
    taps,
    ready,
    strewn,
    swept_0,
    rows,
    rows_high,
    swept_2,
    back_f,
    back_c,
    sent,
    got,
    brought,
):
    arrivals = [
        pltpu.make_async_copy(source, target, brought.at[i])
        for i, (source, target) in enumerate(
            (
                (fine_hbm, fine_ref),
                (upstream_x_hbm, upstream_x),
                (upstream_y_hbm, upstream_y),
                (fractions_hbm, fractions),
                (coarse_hbm, coarse_ref),
            )
        )
    ]
    arrivals[0].start()
    gx, gy = lax.axis_index("gx"), lax.axis_index("gy")
    plane, member = gx // GROUP, lax.rem(gx, GROUP)
    parity = lax.rem(gy, 2)

    def quarter_of(other, odd):
        along = lax.rem(other, 4)
        return along + odd * (1 - 2 * lax.rem(along, 2))

    quarter, level = quarter_of(member, parity), member // 4
    lane = lax.broadcasted_iota(jnp.int32, (8, 128), 1)
    low = lane < HALF
    within = lax.rem(lane, HALF)

    def in_plane(other, gy_step=0):
        return plane * GROUP + other, lax.rem(gy + gy_step + RING, RING)

    def up_planes(step):
        return lax.rem(plane + step + PLANES, PLANES) * GROUP + member, gy

    def mate(step):
        return lax.rem(member + step, GROUP)

    def swap(tile):
        return pltpu.roll(tile, HALF, 1)

    def remote(source, target, channel, device, leave=None):
        leave = channel if leave is None else leave
        return pltpu.make_async_remote_copy(
            source, target, sent.at[leave], got.at[channel], device_id=device, device_id_type=MESH
        )

    def drain(ref, semaphores, channel):
        pltpu.make_async_copy(ref, ref, semaphores.at[channel]).wait()

    barrier = pltpu.get_barrier_semaphore()

    def greet(device):
        pl.semaphore_signal(barrier, inc=1, device_id=device, device_id_type=MESH)

    edge = jnp.logical_or(quarter == 0, quarter == 3)
    outer = jnp.logical_or(member == 0, member == GROUP - 1)
    outward = jnp.where(quarter == 0, -1, 1)
    for step in (3, -3, 2, -2, 1, -1):
        greet(up_planes(step))

    @pl.when(edge)
    def _():
        for other in range(GROUP):
            greet(in_plane(other, outward))

    for step in range(1, GROUP):
        greet(in_plane(mate(step)))
    for arrival in arrivals[1:]:
        arrival.start()

    def pack(field, place):
        for lev in range(2):
            for block in range(2):
                columns = slice(128 * block, 128 * block + 128)
                upper = field[lev, 0:8, columns]
                lower = field[lev, 8:16, columns]
                place(lev, 2 * block, jnp.where(low, upper, swap(lower)))
                place(lev, 2 * block + 1, jnp.where(low, swap(upper), lower))

    def weights_of(pass_row, direction):
        return [taps[2 * pass_row + direction, tap] for tap in range(4)]

    def planes_start(slabs, channel):
        own = slabs.at[3]

        @pl.when(member == GROUP - 1)
        def _():
            remote(own, slabs.at[0], channel, up_planes(3), channel + 4).start()

        @pl.when(member == 0)
        def _():
            remote(own, slabs.at[6], channel, up_planes(-3), channel + 4).start()

        for step in (2, -2, 1, -1):
            remote(own, slabs.at[3 - step], channel, up_planes(step)).start()

    def planes_wait(slabs, channel):
        @pl.when(outer)
        def _():
            drain(slabs.at[pl.ds(0, 5)], got, channel)

        @pl.when(jnp.logical_not(outer))
        def _():
            drain(slabs.at[pl.ds(0, 4)], got, channel)

    def choose(slabs, chosen, pass_row):
        for block in range(2):
            first = (upstream_x[pass_row, 2 * gy + block] - 1 + 16 * OWN) // 16
            slab = (first + lax.rem(member + 1 - first + 48, GROUP) + 7) // 8
            later = jnp.minimum(slab + 1, 6)
            for lev in range(2):
                for half in range(2):
                    tile = 4 * lev + 2 * block + half
                    chosen[tile, 0] = slabs[slab, tile]
                    chosen[tile, 1] = slabs[later, tile]

    def transpose_start(chosen, pencil, channel):
        for step in range(1, GROUP):
            other = mate(step)
            tile = 4 * (other // 4) + quarter_of(other, parity)
            remote(chosen.at[tile], pencil.at[member], channel, in_plane(other)).start()
        pencil[member] = chosen[4 * level + quarter]

    def transpose_wait(pencil, channel):
        drain(pencil.at[pl.ds(0, 7)], got, channel)

    def sweep_x(load, pass_row, block, rows=rows):
        shift = upstream_x[pass_row, block]
        weights = weights_of(pass_row, 0)
        start = shift - 1 + 16 * OWN
        first = start // 16
        return slide([load(first, i) for i in range(10)], start, weights, rows)

    def slide(even_tiles, start, weights, rows=rows):
        count = len(even_tiles) - 2
        odd, inner = lax.rem(start // 8, 2), lax.rem(start, 8)
        swapped = [swap(tile) for tile in even_tiles]
        odd_tiles = [jnp.where(low, swapped[i], swapped[i + 1]) for i in range(count + 1)]
        is_odd = jnp.full((8, 128), odd, jnp.int32) == 1
        lead = [jnp.where(is_odd, odd_tiles[i], even_tiles[i]) for i in range(count + 1)]
        for i in range(count):
            rows[i, 0:8] = lead[i]
            rows[i, 8:16] = jnp.where(is_odd, even_tiles[i + 1], odd_tiles[i])
            rows[i, 16:24] = lead[i + 1]
        sums = []
        for i in range(count):
            summed = weights[0] * rows[i, pl.ds(inner, 8)]
            for tap in range(1, 4):
                summed = summed + weights[tap] * rows[i, pl.ds(inner + tap, 8)]
            sums.append(summed)
        return sums

    def shifted_cells(load, i, offset):
        side = (offset >= 0).astype(jnp.int32)
        turn = offset + HALF * (1 - side)
        return jnp.where(
            within + turn < HALF,
            pltpu.roll(load(i, side), lax.rem(128 - turn, 128), 1),
            pltpu.roll(load(i, side + 1), HALF - turn, 1),
        )

    border = HALF * lax.rem(quarter, 2)
    low_block = lax.rem(2 * gy + (quarter + 1) // 2 - 1 + 2 * RING, 2 * RING)
    high_block = lax.rem(low_block + 1, 2 * RING)

    def crossing_of(to_plane):
        return border - upstream_y[1, to_plane] - 2

    def mix_ahead():
        weights = weights_of(1, 1)
        blank_tile = jnp.zeros((8, 128), jnp.float32)
        kept, split_off = {}, {}
        for side in range(2):
            for tap in range(1, 4):
                split = jnp.logical_and(within + tap >= HALF, lax.rem(quarter, 2) == side)
                kept[side, tap] = jnp.where(split, 0.0, weights[tap])
                split_off[side, tap] = jnp.where(split, weights[tap], 0.0)
        spare = blank_tile
        for i in range(8):
            second = blank_tile
            for side in range(3):
                main = weights[0] * cells[i, side]
                for tap in range(1, 4):
                    moved = pltpu.roll(cells[i, side], 128 - tap, 1)
                    if side == 2:
                        main = main + weights[tap] * moved
                        continue
                    moved = jnp.where(within + tap < HALF, moved, pltpu.roll(cells[i, side + 1], HALF - tap, 1))
                    main = main + kept[side, tap] * moved
                    second = second + split_off[side, tap] * moved
                mixed[i, side] = main
            spare = spare + pltpu.roll(second, (8 * i - 61) % 128, 1)
        return spare

    def sweep_y_ahead(to_plane, tiles, target, at):
        offset = upstream_y[1, to_plane] - 1
        for n, i in enumerate(tiles):
            target[at + n] = shifted_cells(lambda i, side: mixed[i, side], i, offset)
        target[at + len(tiles)] = spare

    def sweep_x_both():
        crossing = crossing_of(plane)
        upper_columns = within > crossing + 2
        both = jnp.logical_and(within >= crossing, within <= crossing + 2)

        def load_low(first, i):
            i = first + i
            place = 9 * ((i + 7) // 8) + lax.rem(i + 7, 8)
            return jnp.where(upper_columns, 0.0, window_1[place])

        def load_high(first, i):
            i = first + i
            level_plane, inside = (i + 7) // 8, lax.rem(i + 7, 8)
            spare = window_1[jnp.where(level_plane == 6, 55, 9 * level_plane + 8)]
            spare = pltpu.roll(spare, lax.rem(crossing - 8 * inside + 256, 128), 1)
            return jnp.where(upper_columns, window_1[9 * level_plane + inside], jnp.where(both, spare, 0.0))

        low_part = sweep_x(load_low, 1, low_block)
        high_part = sweep_x(load_high, 1, high_block, rows_high)
        return [a + b for a, b in zip(low_part, high_part)]

    def sweep_y(pass_row, load, count):
        shift = upstream_y[pass_row, plane]
        weights = weights_of(pass_row, 1)
        sums = [None] * count
        for tap in range(4):
            for i in range(count):
                term = weights[tap] * shifted_cells(load, i, shift - 1 + tap)
                sums[i] = term if sums[i] is None else sums[i] + term
        return sums

    def back_start(swept, back, channel):
        for step in range(1, GROUP):
            other = mate(step)
            remote(swept.at[other], back.at[level, quarter + 1], channel, in_plane(other)).start()
        back[level, quarter + 1] = swept[member]

        @pl.when(edge)
        def _():
            side = jnp.where(quarter == 0, 5, 0)
            for other in range(GROUP):
                remote(swept.at[other], back.at[level, side], channel, in_plane(other, outward), channel + 2).start()

    def back_wait(channel):
        drain(strewn.at[pl.ds(0, 11)], got, channel)

    blank = jnp.zeros((8, 128), jnp.float32)
    for i in (0, 1, 10, 11):
        ready[i] = blank
    for i in range(76):
        strewn[i] = blank

    @pl.when(jnp.logical_and(member > 0, member < 7))
    def _():
        for lev in range(2):
            for part in range(6):
                back_f[lev, part, 5] = blank

    def place_f(lev, part, tile):
        packed_f[lev, part + 1] = tile

    def place_c(lev, part, tile):
        slabs_c[3, 4 * lev + part] = tile

    for lev in range(2):
        packed_f[lev, 0] = jnp.zeros((8, 128), jnp.float32)
        packed_f[lev, 5] = jnp.zeros((8, 128), jnp.float32)
    arrivals[0].wait()
    pack(fine_ref, place_f)
    pl.semaphore_wait(barrier, 17)

    for lev in range(2):
        remote(packed_f.at[lev, 4], edges.at[member], 3, in_plane(4 * lev + 1 - parity, 1)).start()
        remote(packed_f.at[lev, 1], edges.at[member], 3, in_plane(4 * lev + 2 + parity, -1)).start()
    for step in range(1, GROUP):
        other = mate(step)
        source = packed_f.at[other // 4, pl.ds(quarter_of(other, parity), 3)]
        remote(source, cells.at[member], 0, in_plane(other)).start()
    cells[member] = packed_f[level, pl.ds(quarter, 3)]
    arrivals[4].wait()
    pack(coarse_ref, place_c)
    planes_start(slabs_c, 1)
    for arrival in arrivals[1:4]:
        arrival.wait()
    for pass_row in range(3):
        for direction in range(2):
            for tap, weight in enumerate(cubic_weights(fractions[direction, pass_row])):
                taps[2 * pass_row + direction, tap] = weight
    drain(cells.at[pl.ds(0, 7)], got, 0)

    @pl.when(edge)
    def _():
        drain(edges, got, 3)
        side = jnp.where(quarter == 0, 0, 2)
        for i in range(8):
            cells[i, side] = edges[i]

    def to(step):
        return lax.rem(plane + step + PLANES, PLANES)

    spare = mix_ahead()
    def send_ahead(n, step):
        sweep_y_ahead(to(step), range(8), ahead, 9 * n)
        target = window_1.at[pl.ds(9 * (3 - step), 9)]
        remote(ahead.at[pl.ds(9 * n, 9)], target, 2, up_planes(step)).start()

    send_ahead(0, 2)
    send_ahead(1, -2)
    sweep_y_ahead(to(3), (7,), fringe, 0)
    remote(fringe.at[pl.ds(0, 2)], window_1.at[pl.ds(7, 2)], 2, up_planes(3)).start()
    sweep_y_ahead(to(-3), (0,), fringe, 2)
    remote(fringe.at[pl.ds(2, 2)], window_1.at[pl.ds(54, 2)], 2, up_planes(-3)).start()
    send_ahead(2, 1)
    send_ahead(3, -1)
    sweep_y_ahead(plane, range(8), window_1, 27)
    planes_wait(slabs_c, 1)
    choose(slabs_c, chosen_c, 2)
    transpose_start(chosen_c, pencil_c, 4)
    own_block = 2 * gy + quarter // 2
    transpose_wait(pencil_c, 4)
    coarse_rows = sweep_x(lambda first, i: pencil_c[lax.rem(first + i + 7, 8), i // 8], 2, own_block)
    for i, tile in enumerate(coarse_rows):
        swept_2[i] = tile
    back_start(swept_2, back_c, 6)

    drain(window_1.at[pl.ds(0, 40)], got, 2)

    for i, tile in enumerate(sweep_x_both()):
        ready[2 + i] = tile
    start = upstream_x[0, own_block] - 1 + 16 * OWN
    parts = slide([ready[i] for i in range(12)], start, weights_of(0, 0))
    for i, tile in enumerate(parts):
        strewn[32 + i] = tile
    for i in range(WINDOW):
        swept_0[i] = strewn[start // 16 + i]

    def scatter_start(step, others, slot, outer_gy):
        def start_at(gy_step, side, leave, skip):
            for other in others:
                target_plane = lax.rem(plane - step + PLANES, PLANES)
                copy = remote(
                    swept_0.at[OWN - 8 * step + other],
                    back_f.at[level, side, slot],
                    7,
                    (target_plane * GROUP + other, lax.rem(gy + gy_step + RING, RING)),
                    leave,
                )
                if skip:
                    pl.when(other != member)(copy.start)
                else:
                    copy.start()

        if outer_gy:
            @pl.when(edge)
            def _():
                start_at(outward, jnp.where(quarter == 0, 5, 0), 9, False)
        else:
            start_at(0, quarter + 1, 7, step == 0)

    for outer_gy in (True, False):
        scatter_start(3, (7,), 5, outer_gy)
        scatter_start(-3, (0,), 5, outer_gy)
    for outer_gy in (True, False):
        for step in (2, -2, 1, -1, 0):
            scatter_start(step, range(GROUP), step + 2, outer_gy)
    back_f[level, quarter + 1, 2] = swept_0[OWN + member]

    back_wait(6)
    coarse = sweep_y(2, lambda i, side: back_c[i // 4, lax.rem(i, 4) + side], 8)

    drain(cells.at[pl.ds(0, 7)], sent, 0)
    drain(slabs_c.at[pl.ds(0, 4)], sent, 1)

    @pl.when(outer)
    def _():
        drain(slabs_c.at[0], sent, 5)

    drain(strewn.at[pl.ds(0, 4)], sent, 3)
    drain(window_1.at[pl.ds(0, 40)], sent, 2)
    drain(pencil_c.at[pl.ds(0, 7)], sent, 4)
    drain(strewn.at[pl.ds(0, 7)], sent, 6)
    drain(strewn.at[pl.ds(0, 41)], sent, 7)

    @pl.when(edge)
    def _():
        drain(strewn.at[pl.ds(0, 8)], sent, 8)
        drain(strewn.at[pl.ds(0, 42)], sent, 9)

    @pl.when(outer)
    def _():
        drain(strewn.at[pl.ds(0, 71)], got, 7)

    @pl.when(jnp.logical_not(outer))
    def _():
        drain(strewn.at[pl.ds(0, 59)], got, 7)

    for lev in range(2):
        for part in range(6):
            total = back_f[lev, part, 0]
            for slot in range(1, 6):
                total = total + back_f[lev, part, slot]
            ready[lev * 6 + part] = total
    fine = sweep_y(0, lambda i, side: ready[6 * (i // 4) + lax.rem(i, 4) + side], 8)
    tiles = [a - b for a, b in zip(fine, coarse)]
    for lev in range(2):
        for block in range(2):
            columns = slice(128 * block, 128 * block + 128)
            even, odd = tiles[lev * 4 + 2 * block], tiles[lev * 4 + 2 * block + 1]
            out_ref[lev, 0:8, columns] = jnp.where(low, even, swap(odd))
            out_ref[lev, 8:16, columns] = jnp.where(low, swap(even), odd)


def local(fine_cotangent, coarse_cotangent, upstream_x, upstream_y, fractions):
    vmem = pl.BlockSpec(memory_space=pltpu.VMEM)
    anywhere = pl.BlockSpec(memory_space=pl.ANY)

    def tiles(*shape):
        return pltpu.VMEM((*shape, 8, 128), jnp.float32)

    return pl.pallas_call(
        kernel,
        out_shape=pltpu.VMEM(fine_cotangent.shape, jnp.float32),
        in_specs=[anywhere] * 5,
        out_specs=vmem,
        scratch_shapes=[
            pltpu.VMEM(fine_cotangent.shape, jnp.float32),
            pltpu.VMEM(fine_cotangent.shape, jnp.float32),
            pltpu.SMEM(upstream_x.shape, jnp.int32),
            pltpu.SMEM(upstream_y.shape, jnp.int32),
            pltpu.SMEM((2, 3), jnp.float32),
            tiles(2, 6),
            tiles(7, 8),
            tiles(8, 2),
            tiles(8, 2),
            tiles(8, 3),
            tiles(8, 3),
            tiles(8),
            tiles(36),
            tiles(4),
            tiles(63),
            tiles(6, 4),
            tiles(12),
            tiles(76),
            tiles(WINDOW),
            pltpu.VMEM((10, 24, 128), jnp.float32),
            pltpu.VMEM((10, 24, 128), jnp.float32),
            tiles(8),
            tiles(2, 6, 6),
            tiles(2, 6),
            pltpu.SemaphoreType.DMA((10,)),
            pltpu.SemaphoreType.DMA((8,)),
            pltpu.SemaphoreType.DMA((5,)),
        ],
        compiler_params=pltpu.CompilerParams(collective_id=0, has_side_effects=True),
    )(fine_cotangent, coarse_cotangent, upstream_x, upstream_y, fractions.T)


def solution(mesh):
    placed = (P(None, "gx", "gy"), P(None, "gx", "gy"), P(), P(), P())
    return jax.shard_map(
        local, mesh=mesh, in_specs=placed, out_specs=P(None, "gx", "gy"), check_vma=False
    )
```

```python
import jax
import jax.numpy as jnp
from jax import lax
from jax.experimental import pallas as pl
from jax.experimental.pallas import tpu as pltpu
from jax.sharding import PartitionSpec as P

MESH = pl.DeviceIdType.MESH
PLANES = 16
GROUP = 8
RING = 4
HALF = 64
OWN = 17
WINDOW = 42


def cubic_weights(fraction):
    position = 1.0 - jnp.full((8, 128), fraction, jnp.float32)
    taps = (
        -position * (position - 1.0) * (position - 2.0) / 6.0,
        (position + 1.0) * (position - 1.0) * (position - 2.0) / 2.0,
        -(position + 1.0) * position * (position - 2.0) / 2.0,
        (position + 1.0) * position * (position - 1.0) / 6.0,
    )
    return taps[::-1]


def kernel(
    fine_hbm,
    coarse_hbm,
    upstream_x_hbm,
    upstream_y_hbm,
    fractions_hbm,
    out_ref,
    fine_ref,
    coarse_ref,
    upstream_x,
    upstream_y,
    fractions,
    packed_f,
    slabs_c,
    chosen_c,
    pencil_c,
    cells,
    mixed,
    edges,
    ahead,
    fringe,
    window_1,
    taps,
    ready,
    strewn,
    swept_0,
    rows,
    rows_high,
    swept_2,
    back_f,
    back_c,
    sent,
    got,
    brought,
):
    arrivals = [
        pltpu.make_async_copy(source, target, brought.at[i])
        for i, (source, target) in enumerate(
            (
                (fine_hbm, fine_ref),
                (upstream_x_hbm, upstream_x),
                (upstream_y_hbm, upstream_y),
                (fractions_hbm, fractions),
                (coarse_hbm, coarse_ref),
            )
        )
    ]
    arrivals[0].start()
    gx, gy = lax.axis_index("gx"), lax.axis_index("gy")
    plane, member = gx // GROUP, lax.rem(gx, GROUP)
    parity = lax.rem(gy, 2)

    def quarter_of(other, odd):
        along = lax.rem(other, 4)
        return along + odd * (1 - 2 * lax.rem(along, 2))

    quarter, level = quarter_of(member, parity), member // 4
    lane = lax.broadcasted_iota(jnp.int32, (8, 128), 1)
    low = lane < HALF
    within = lax.rem(lane, HALF)

    def in_plane(other, gy_step=0):
        return plane * GROUP + other, lax.rem(gy + gy_step + RING, RING)

    def up_planes(step):
        return lax.rem(plane + step + PLANES, PLANES) * GROUP + member, gy

    def mate(step):
        return lax.rem(member + step, GROUP)

    def swap(tile):
        return pltpu.roll(tile, HALF, 1)

    def remote(source, target, channel, device, leave=None):
        leave = channel if leave is None else leave
        return pltpu.make_async_remote_copy(
            source, target, sent.at[leave], got.at[channel], device_id=device, device_id_type=MESH
        )

    def drain(ref, semaphores, channel):
        pltpu.make_async_copy(ref, ref, semaphores.at[channel]).wait()

    barrier = pltpu.get_barrier_semaphore()

    def greet(device):
        pl.semaphore_signal(barrier, inc=1, device_id=device, device_id_type=MESH)

    edge = jnp.logical_or(quarter == 0, quarter == 3)
    outer = jnp.logical_or(member == 0, member == GROUP - 1)
    outward = jnp.where(quarter == 0, -1, 1)
    for step in (3, -3, 2, -2, 1, -1):
        greet(up_planes(step))

    @pl.when(edge)
    def _():
        for other in range(GROUP):
            greet(in_plane(other, outward))

    for step in range(1, GROUP):
        greet(in_plane(mate(step)))
    for arrival in arrivals[1:]:
        arrival.start()

    def pack(field, place):
        for lev in range(2):
            for block in range(2):
                columns = slice(128 * block, 128 * block + 128)
                upper = field[lev, 0:8, columns]
                lower = field[lev, 8:16, columns]
                place(lev, 2 * block, jnp.where(low, upper, swap(lower)))
                place(lev, 2 * block + 1, jnp.where(low, swap(upper), lower))

    def weights_of(pass_row, direction):
        return [taps[2 * pass_row + direction, tap] for tap in range(4)]

    def planes_start(slabs, channel):
        own = slabs.at[3]

        @pl.when(member == GROUP - 1)
        def _():
            remote(own, slabs.at[0], channel, up_planes(3), channel + 4).start()

        @pl.when(member == 0)
        def _():
            remote(own, slabs.at[6], channel, up_planes(-3), channel + 4).start()

        for step in (2, -2, 1, -1):
            remote(own, slabs.at[3 - step], channel, up_planes(step)).start()

    def planes_wait(slabs, channel):
        @pl.when(outer)
        def _():
            drain(slabs.at[pl.ds(0, 5)], got, channel)

        @pl.when(jnp.logical_not(outer))
        def _():
            drain(slabs.at[pl.ds(0, 4)], got, channel)

    def choose(slabs, chosen, pass_row):
        for block in range(2):
            first = (upstream_x[pass_row, 2 * gy + block] - 1 + 16 * OWN) // 16
            slab = (first + lax.rem(member + 1 - first + 48, GROUP) + 7) // 8
            later = jnp.minimum(slab + 1, 6)
            for lev in range(2):
                for half in range(2):
                    tile = 4 * lev + 2 * block + half
                    chosen[tile, 0] = slabs[slab, tile]
                    chosen[tile, 1] = slabs[later, tile]

    def transpose_start(chosen, pencil, channel):
        for step in range(1, GROUP):
            other = mate(step)
            tile = 4 * (other // 4) + quarter_of(other, parity)
            remote(chosen.at[tile], pencil.at[member], channel, in_plane(other)).start()
        pencil[member] = chosen[4 * level + quarter]

    def transpose_wait(pencil, channel):
        drain(pencil.at[pl.ds(0, 7)], got, channel)

    def sweep_x(load, pass_row, block, rows=rows):
        shift = upstream_x[pass_row, block]
        weights = weights_of(pass_row, 0)
        start = shift - 1 + 16 * OWN
        first = start // 16
        return slide([load(first, i) for i in range(10)], start, weights, rows)

    def slide(even_tiles, start, weights, rows=rows):
        count = len(even_tiles) - 2
        odd, inner = lax.rem(start // 8, 2), lax.rem(start, 8)
        swapped = [swap(tile) for tile in even_tiles]
        odd_tiles = [jnp.where(low, swapped[i], swapped[i + 1]) for i in range(count + 1)]
        is_odd = jnp.full((8, 128), odd, jnp.int32) == 1
        lead = [jnp.where(is_odd, odd_tiles[i], even_tiles[i]) for i in range(count + 1)]
        for i in range(count):
            rows[i, 0:8] = lead[i]
            rows[i, 8:16] = jnp.where(is_odd, even_tiles[i + 1], odd_tiles[i])
            rows[i, 16:24] = lead[i + 1]
        sums = []
        for i in range(count):
            summed = weights[0] * rows[i, pl.ds(inner, 8)]
            for tap in range(1, 4):
                summed = summed + weights[tap] * rows[i, pl.ds(inner + tap, 8)]
            sums.append(summed)
        return sums

    def shifted_cells(load, i, offset):
        side = (offset >= 0).astype(jnp.int32)
        turn = offset + HALF * (1 - side)
        return jnp.where(
            within + turn < HALF,
            pltpu.roll(load(i, side), lax.rem(128 - turn, 128), 1),
            pltpu.roll(load(i, side + 1), HALF - turn, 1),
        )

    border = HALF * lax.rem(quarter, 2)
    low_block = lax.rem(2 * gy + (quarter + 1) // 2 - 1 + 2 * RING, 2 * RING)
    high_block = lax.rem(low_block + 1, 2 * RING)

    def crossing_of(to_plane):
        return border - upstream_y[1, to_plane] - 2

    def mix_ahead():
        weights = weights_of(1, 1)
        blank_tile = jnp.zeros((8, 128), jnp.float32)
        kept, split_off = {}, {}
        for side in range(2):
            for tap in range(1, 4):
                split = jnp.logical_and(within + tap >= HALF, lax.rem(quarter, 2) == side)
                kept[side, tap] = jnp.where(split, 0.0, weights[tap])
                split_off[side, tap] = jnp.where(split, weights[tap], 0.0)
        spare = blank_tile
        for i in range(8):
            second = blank_tile
            for side in range(3):
                main = weights[0] * cells[i, side]
                for tap in range(1, 4):
                    moved = pltpu.roll(cells[i, side], 128 - tap, 1)
                    if side == 2:
                        main = main + weights[tap] * moved
                        continue
                    moved = jnp.where(within + tap < HALF, moved, pltpu.roll(cells[i, side + 1], HALF - tap, 1))
                    main = main + kept[side, tap] * moved
                    second = second + split_off[side, tap] * moved
                mixed[i, side] = main
            spare = spare + pltpu.roll(second, (8 * i - 61) % 128, 1)
        return spare

    def sweep_y_ahead(to_plane, tiles, target, at):
        offset = upstream_y[1, to_plane] - 1
        for n, i in enumerate(tiles):
            target[at + n] = shifted_cells(lambda i, side: mixed[i, side], i, offset)
        target[at + len(tiles)] = spare

    def sweep_x_both():
        crossing = crossing_of(plane)
        upper_columns = within > crossing + 2
        both = jnp.logical_and(within >= crossing, within <= crossing + 2)

        def load_low(first, i):
            i = first + i
            place = 9 * ((i + 7) // 8) + lax.rem(i + 7, 8)
            return jnp.where(upper_columns, 0.0, window_1[place])

        def load_high(first, i):
            i = first + i
            level_plane, inside = (i + 7) // 8, lax.rem(i + 7, 8)
            spare = window_1[jnp.where(level_plane == 6, 55, 9 * level_plane + 8)]
            spare = pltpu.roll(spare, lax.rem(crossing - 8 * inside + 256, 128), 1)
            return jnp.where(upper_columns, window_1[9 * level_plane + inside], jnp.where(both, spare, 0.0))

        low_part = sweep_x(load_low, 1, low_block)
        high_part = sweep_x(load_high, 1, high_block, rows_high)
        return [a + b for a, b in zip(low_part, high_part)]

    def sweep_y(pass_row, load, count):
        shift = upstream_y[pass_row, plane]
        weights = weights_of(pass_row, 1)
        sums = [None] * count
        for tap in range(4):
            for i in range(count):
                term = weights[tap] * shifted_cells(load, i, shift - 1 + tap)
                sums[i] = term if sums[i] is None else sums[i] + term
        return sums

    def back_start(swept, back, channel):
        for step in range(1, GROUP):
            other = mate(step)
            remote(swept.at[other], back.at[level, quarter + 1], channel, in_plane(other)).start()
        back[level, quarter + 1] = swept[member]

        @pl.when(edge)
        def _():
            side = jnp.where(quarter == 0, 5, 0)
            for other in range(GROUP):
                remote(swept.at[other], back.at[level, side], channel, in_plane(other, outward), channel + 2).start()

    def back_wait(channel):
        drain(strewn.at[pl.ds(0, 11)], got, channel)

    blank = jnp.zeros((8, 128), jnp.float32)

    def place_f(lev, part, tile):
        packed_f[lev, part + 1] = tile

    def place_c(lev, part, tile):
        slabs_c[3, 4 * lev + part] = tile

    for lev in range(2):
        packed_f[lev, 0] = jnp.zeros((8, 128), jnp.float32)
        packed_f[lev, 5] = jnp.zeros((8, 128), jnp.float32)
    arrivals[0].wait()
    pack(fine_ref, place_f)
    pl.semaphore_wait(barrier, 17)

    for lev in range(2):
        remote(packed_f.at[lev, 4], edges.at[member], 3, in_plane(4 * lev + 1 - parity, 1)).start()
        remote(packed_f.at[lev, 1], edges.at[member], 3, in_plane(4 * lev + 2 + parity, -1)).start()
    for step in range(1, GROUP):
        other = mate(step)
        source = packed_f.at[other // 4, pl.ds(quarter_of(other, parity), 3)]
        remote(source, cells.at[member], 0, in_plane(other)).start()
    cells[member] = packed_f[level, pl.ds(quarter, 3)]
    arrivals[4].wait()
    pack(coarse_ref, place_c)
    planes_start(slabs_c, 1)
    for i in (0, 1, 10, 11):
        ready[i] = blank
    for i in range(76):
        strewn[i] = blank

    @pl.when(jnp.logical_and(member > 0, member < 7))
    def _():
        for lev in range(2):
            for part in range(6):
                back_f[lev, part, 5] = blank

    for arrival in arrivals[1:4]:
        arrival.wait()
    for pass_row in range(3):
        for direction in range(2):
            for tap, weight in enumerate(cubic_weights(fractions[direction, pass_row])):
                taps[2 * pass_row + direction, tap] = weight
    drain(cells.at[pl.ds(0, 7)], got, 0)

    @pl.when(edge)
    def _():
        drain(edges, got, 3)
        side = jnp.where(quarter == 0, 0, 2)
        for i in range(8):
            cells[i, side] = edges[i]

    def to(step):
        return lax.rem(plane + step + PLANES, PLANES)

    spare = mix_ahead()
    def send_ahead(n, step):
        sweep_y_ahead(to(step), range(8), ahead, 9 * n)
        target = window_1.at[pl.ds(9 * (3 - step), 9)]
        remote(ahead.at[pl.ds(9 * n, 9)], target, 2, up_planes(step)).start()

    send_ahead(0, 2)
    send_ahead(1, -2)
    sweep_y_ahead(to(3), (7,), fringe, 0)
    remote(fringe.at[pl.ds(0, 2)], window_1.at[pl.ds(7, 2)], 2, up_planes(3)).start()
    sweep_y_ahead(to(-3), (0,), fringe, 2)
    remote(fringe.at[pl.ds(2, 2)], window_1.at[pl.ds(54, 2)], 2, up_planes(-3)).start()
    send_ahead(2, 1)
    send_ahead(3, -1)
    sweep_y_ahead(plane, range(8), window_1, 27)
    planes_wait(slabs_c, 1)
    choose(slabs_c, chosen_c, 2)
    transpose_start(chosen_c, pencil_c, 4)
    own_block = 2 * gy + quarter // 2
    transpose_wait(pencil_c, 4)
    coarse_rows = sweep_x(lambda first, i: pencil_c[lax.rem(first + i + 7, 8), i // 8], 2, own_block)
    for i, tile in enumerate(coarse_rows):
        swept_2[i] = tile
    back_start(swept_2, back_c, 6)

    drain(window_1.at[pl.ds(0, 40)], got, 2)

    for i, tile in enumerate(sweep_x_both()):
        ready[2 + i] = tile
    start = upstream_x[0, own_block] - 1 + 16 * OWN
    parts = slide([ready[i] for i in range(12)], start, weights_of(0, 0))
    for i, tile in enumerate(parts):
        strewn[32 + i] = tile
    for i in range(WINDOW):
        swept_0[i] = strewn[start // 16 + i]

    def scatter_start(step, others, slot, outer_gy):
        def start_at(gy_step, side, leave, skip):
            for other in others:
                target_plane = lax.rem(plane - step + PLANES, PLANES)
                copy = remote(
                    swept_0.at[OWN - 8 * step + other],
                    back_f.at[level, side, slot],
                    7,
                    (target_plane * GROUP + other, lax.rem(gy + gy_step + RING, RING)),
                    leave,
                )
                if skip:
                    pl.when(other != member)(copy.start)
                else:
                    copy.start()

        if outer_gy:
            @pl.when(edge)
            def _():
                start_at(outward, jnp.where(quarter == 0, 5, 0), 9, False)
        else:
            start_at(0, quarter + 1, 7, step == 0)

    for outer_gy in (True, False):
        scatter_start(3, (7,), 5, outer_gy)
        scatter_start(-3, (0,), 5, outer_gy)
    for outer_gy in (True, False):
        for step in (2, -2, 1, -1, 0):
            scatter_start(step, range(GROUP), step + 2, outer_gy)
    back_f[level, quarter + 1, 2] = swept_0[OWN + member]

    back_wait(6)
    coarse = sweep_y(2, lambda i, side: back_c[i // 4, lax.rem(i, 4) + side], 8)

    drain(cells.at[pl.ds(0, 7)], sent, 0)
    drain(slabs_c.at[pl.ds(0, 4)], sent, 1)

    @pl.when(outer)
    def _():
        drain(slabs_c.at[0], sent, 5)

    drain(strewn.at[pl.ds(0, 4)], sent, 3)
    drain(window_1.at[pl.ds(0, 40)], sent, 2)
    drain(pencil_c.at[pl.ds(0, 7)], sent, 4)
    drain(strewn.at[pl.ds(0, 7)], sent, 6)
    drain(strewn.at[pl.ds(0, 41)], sent, 7)

    @pl.when(edge)
    def _():
        drain(strewn.at[pl.ds(0, 8)], sent, 8)
        drain(strewn.at[pl.ds(0, 42)], sent, 9)

    @pl.when(outer)
    def _():
        drain(strewn.at[pl.ds(0, 71)], got, 7)

    @pl.when(jnp.logical_not(outer))
    def _():
        drain(strewn.at[pl.ds(0, 59)], got, 7)

    for lev in range(2):
        for part in range(6):
            total = back_f[lev, part, 0]
            for slot in range(1, 6):
                total = total + back_f[lev, part, slot]
            ready[lev * 6 + part] = total
    fine = sweep_y(0, lambda i, side: ready[6 * (i // 4) + lax.rem(i, 4) + side], 8)
    tiles = [a - b for a, b in zip(fine, coarse)]
    for lev in range(2):
        for block in range(2):
            columns = slice(128 * block, 128 * block + 128)
            even, odd = tiles[lev * 4 + 2 * block], tiles[lev * 4 + 2 * block + 1]
            out_ref[lev, 0:8, columns] = jnp.where(low, even, swap(odd))
            out_ref[lev, 8:16, columns] = jnp.where(low, swap(even), odd)


def local(fine_cotangent, coarse_cotangent, upstream_x, upstream_y, fractions):
    vmem = pl.BlockSpec(memory_space=pltpu.VMEM)
    anywhere = pl.BlockSpec(memory_space=pl.ANY)

    def tiles(*shape):
        return pltpu.VMEM((*shape, 8, 128), jnp.float32)

    return pl.pallas_call(
        kernel,
        out_shape=pltpu.VMEM(fine_cotangent.shape, jnp.float32),
        in_specs=[anywhere] * 5,
        out_specs=vmem,
        scratch_shapes=[
            pltpu.VMEM(fine_cotangent.shape, jnp.float32),
            pltpu.VMEM(fine_cotangent.shape, jnp.float32),
            pltpu.SMEM(upstream_x.shape, jnp.int32),
            pltpu.SMEM(upstream_y.shape, jnp.int32),
            pltpu.SMEM((2, 3), jnp.float32),
            tiles(2, 6),
            tiles(7, 8),
            tiles(8, 2),
            tiles(8, 2),
            tiles(8, 3),
            tiles(8, 3),
            tiles(8),
            tiles(36),
            tiles(4),
            tiles(63),
            tiles(6, 4),
            tiles(12),
            tiles(76),
            tiles(WINDOW),
            pltpu.VMEM((10, 24, 128), jnp.float32),
            pltpu.VMEM((10, 24, 128), jnp.float32),
            tiles(8),
            tiles(2, 6, 6),
            tiles(2, 6),
            pltpu.SemaphoreType.DMA((10,)),
            pltpu.SemaphoreType.DMA((8,)),
            pltpu.SemaphoreType.DMA((5,)),
        ],
        compiler_params=pltpu.CompilerParams(collective_id=0, has_side_effects=True),
    )(fine_cotangent, coarse_cotangent, upstream_x, upstream_y, fractions.T)


def solution(mesh):
    placed = (P(None, "gx", "gy"), P(None, "gx", "gy"), P(), P(), P())
    return jax.shard_map(
        local, mesh=mesh, in_specs=placed, out_specs=P(None, "gx", "gy"), check_vma=False
    )
```
